32 devices in a mesh: groups: 2 (over y), orb: 4 (over z), fit: 2 (over x), rep: 2 (over core).
Axes of the slice: x: 2, y: 2, z: 4, core: 2. Of those that a mesh axis runs over, the one named last changes fastest.
Arguments:
- blocks: bfloat16 [64, 2048, 256], P(('groups', 'orb'), 'fit'), parts along dimension 0, may hold values from -0.8984375 to 0.8984375
- occ_energy: bfloat16 [64], P(('groups', 'orb')), parts along dimension 0, may hold values from -2 to -0.5
- pair_list: int32 [128, 2], P(('groups', 'orb', 'rep')), parts along dimension 0, may hold values from 0 to 31, as said below
- pno_sizes: int32 [128], P(('groups', 'orb', 'rep')), parts along dimension 0, may hold values from 64 to 256
- fock_virt: float32 [128, 256, 256], P(('groups', 'orb', 'rep')), parts along dimension 0, as said below
Outputs:
- amplitudes: bfloat16 [128, 256, 256], P(('groups', 'orb', 'rep')), parts along dimension 0
- grads: float32 [64, 2048, 256], P(('groups', 'orb'), 'fit'), parts along dimension 0
The draws below stay inside these ranges and needn't reach their ends.
There are 2 independent parts, one for each index of `groups`. The reference program is written for one: setup_inputs(seed, part) draws one part's arguments, and reference() takes and returns one part's arrays. A program takes and returns all parts, laid end to end along the dimension named above; each array names one. Nothing has to cross between parts.
Inputs may be any that keep to these rules, and one draw needn't show every extreme that they name: `pair_list`: each row names two different orbitals; orbital g lies on orb index g // 8. Among the orbitals named by one device's 8 rows (aligned blocks of 8 rows), at most 2 distinct ones lie on any one orb index, and for every device exactly 2 lie on some orb index. `fock_virt`: symmetric with a positive diagonal.
All inputs are finite; a program needn't handle non-finite values.
Results may differ from the reference program's by a relative error of at most 0.014.
Values may be sent and summed in bfloat16 or wider, within the bound.
No kernel may reach another device: no remote copies, remote signals or barrier semaphores. Data moves between devices by JAX's collectives and lax.ppermute only.
A program may use at most 128 MiB of HBM per device.

```python
import math
import jax
import jax.numpy as jnp
from jax import lax

NAUX = 2048
V = 256
ORB_DEV = 8
PAIR_DEV = 8
CAP = 2
ITERS = 2
ORBS = 32
PAIRS = 64


def draw_pair_list(key, part):
    key = jax.random.fold_in(key, 11)
    owners = PAIRS // PAIR_DEV
    sources = ORBS // ORB_DEV
    candidates_count = sources * CAP
    key_order, key_first, key_offset = jax.random.split(key, 3)
    scores = jax.random.randint(key_order, (owners, sources, ORB_DEV), 0, 2 ** 20)
    scores = scores * ORB_DEV + jnp.arange(ORB_DEV, dtype=jnp.int32)[None, None, :]
    chosen = jnp.argsort(scores, axis=-1)[:, :, :CAP].astype(jnp.int32)
    candidates = (jnp.arange(sources, dtype=jnp.int32)[None, :, None] * ORB_DEV + chosen).reshape(owners, candidates_count)
    first = jax.random.randint(key_first, (owners, PAIR_DEV), 0, candidates_count)
    offset = jax.random.randint(key_offset, (owners, PAIR_DEV), 1, candidates_count)
    second = (first + offset) % candidates_count
    first = first.at[:, 0].set(0)
    second = second.at[:, 0].set(1)
    left = jnp.take_along_axis(candidates, first, axis=1)
    right = jnp.take_along_axis(candidates, second, axis=1)
    return jnp.stack([left, right], axis=-1).reshape(PAIRS, 2).astype(jnp.int32)


def draw_fock_virt(key, part):
    key = jax.random.fold_in(key, 7)
    key_diag, key_off = jax.random.split(key)
    lowest, highest = (1.0, 8.0)
    diagonal = jnp.exp(jax.random.uniform(key_diag, (PAIRS, V), jnp.float32, math.log(lowest), math.log(highest)))
    raw = jax.random.uniform(key_off, (PAIRS, V, V), jnp.float32, -1.0, 1.0)
    symmetric = (raw + jnp.swapaxes(raw, 1, 2)) * (0.6 / math.sqrt(2.0 * V))
    scales = jnp.sqrt(diagonal[:, :, None] * diagonal[:, None, :])
    identity = jnp.arange(V)[:, None] == jnp.arange(V)[None, :]
    on_diag = diagonal[:, :, None] * jnp.ones((1, 1, V), jnp.float32)
    full = jnp.where(identity[None, :, :], on_diag, symmetric * scales)
    return full.astype(jnp.float32)


def with_ends(drawn, rng, least, high):
    dims = drawn.shape
    index_at = [jax.random.randint(jax.random.fold_in(rng, axis), (), 0, dims[axis]) for axis in range(len(dims))]
    drawn = drawn.at[tuple(index_at)].set(least)
    longest = dims.index(max(dims))
    index_at[longest] = (index_at[longest] + 1) % dims[longest]
    return drawn.at[tuple(index_at)].set(high)


def shard_levels(rng, shape, shards, low, high):
    level, own = 1.0, jax.random.fold_in(rng, 6)
    for axis_at, shards_of in shards:
        heights = jnp.exp(jax.random.uniform(jax.random.fold_in(own, axis_at), (shards_of,), jnp.float32, low / len(shards), high / len(shards)))
        level = level * jnp.repeat(heights, shape[axis_at] // shards_of).reshape([-1 if axis == axis_at else 1 for axis in range(len(shape))])
    return level


def normal_values(rng, dims, deviation, bound, shards=(), kind=jnp.bfloat16):
    values = jax.random.normal(rng, dims, jnp.float32) * deviation
    if len(shards) > 0:
        values = shard_levels(rng, dims, shards, -0.22, 0.18) * values
    return jnp.clip(values, min=-bound, max=bound).astype(kind)


def setup_inputs(seed: int = 0, part: int = 0) -> dict:
    key_of = jax.random.split(jax.random.key(seed), 6)
    part_splits = jax.random.split(jax.random.fold_in(key_of[5], part), 6)
    return {
        "blocks": normal_values(part_splits[0], (ORBS, NAUX, V), 0.15, 0.8984375, ((0, 4), (1, 2))),
        "occ_energy": jnp.clip(-2.0 + 1.5 * jax.random.uniform(part_splits[1], (ORBS,), jnp.float32) ** shard_levels(part_splits[1], (ORBS,), ((0, 4),), -0.2, 0.2), -2.0, -0.5).astype(jnp.bfloat16),
        "pair_list": draw_pair_list(jax.random.fold_in(jax.random.fold_in(key_of[5], part), 71), part),
        "pno_sizes": with_ends(jax.random.randint(part_splits[3], (PAIRS,), V // 4, V + 1), jax.random.fold_in(part_splits[3], 1), V // 4, V).astype(jnp.int32),
        "fock_virt": draw_fock_virt(jax.random.fold_in(jax.random.fold_in(key_of[5], part), 71), part),
    }


def iterate_pairs(exchange_ints, fock_here, occ_sums, pno_mask):
    diagonal = jnp.diagonal(fock_here, axis1=1, axis2=2)
    denominator = diagonal[:, :, None] + diagonal[:, None, :] - occ_sums[:, None, None]
    current = jnp.zeros_like(exchange_ints)
    for iteration in range(ITERS):
        left_term = jnp.einsum("pab,pbc->pac", fock_here, current, precision=lax.Precision.HIGHEST)
        right_term = jnp.einsum("pab,pbc->pac", current, fock_here, precision=lax.Precision.HIGHEST)
        residual = (exchange_ints + left_term + right_term - occ_sums[:, None, None] * current) * pno_mask
        current = current - residual / denominator
    return current.astype(jnp.bfloat16)


def reference(blocks, occ_energy, pair_list, pno_sizes, fock_virt):
    owners = PAIRS // PAIR_DEV

    def owner_step(grads_sum, inputs):
        pairs_here, sizes_here, fock_here = inputs
        left_index = pairs_here[:, 0]
        right_index = pairs_here[:, 1]
        left_blocks = blocks[left_index].astype(jnp.float32)
        right_blocks = blocks[right_index].astype(jnp.float32)
        occ_sums = occ_energy[left_index].astype(jnp.float32) + occ_energy[right_index].astype(jnp.float32)
        pno_rows = (jnp.arange(V, dtype=jnp.int32)[None, :] < sizes_here[:, None]).astype(jnp.float32)
        pno_mask = pno_rows[:, :, None] * pno_rows[:, None, :]
        exchange_ints = jnp.einsum("pfa,pfb->pab", left_blocks, right_blocks) * pno_mask
        amplitudes = iterate_pairs(exchange_ints, fock_here, occ_sums, pno_mask)
        amp_float = amplitudes.astype(jnp.float32)
        weighted = (2.0 * amp_float - jnp.swapaxes(amp_float, 1, 2)).astype(jnp.bfloat16).astype(jnp.float32)
        left_grad = jnp.einsum("pfb,pab->pfa", right_blocks, weighted)
        right_grad = jnp.einsum("pfa,pab->pfb", left_blocks, weighted)
        contributions = jnp.stack([left_grad, right_grad], axis=1).reshape(2 * PAIR_DEV, NAUX, V)
        endpoints = pairs_here.reshape(-1).astype(jnp.int32)
        partial_sum = jnp.zeros((ORBS, NAUX, V), jnp.float32).at[endpoints].add(contributions)
        rounded = lax.optimization_barrier(partial_sum.astype(jnp.bfloat16))
        return grads_sum + rounded.astype(jnp.float32), amplitudes

    inputs = (pair_list.reshape(owners, PAIR_DEV, 2), pno_sizes.reshape(owners, PAIR_DEV), fock_virt.reshape(owners, PAIR_DEV, V, V))
    grads, amplitudes = lax.scan(owner_step, jnp.zeros((ORBS, NAUX, V), jnp.float32), inputs)
    return amplitudes.reshape(PAIRS, V, V), grads
```

```python
import functools

import jax
import jax.numpy as jnp
from jax import lax
from jax.experimental import pallas as pl
from jax.experimental.pallas import tpu as pltpu
from jax.sharding import PartitionSpec as P

CAP = 2
FORWARD_CHUNKS = 2
BACK_CHUNKS = 4
VMEM_LIMIT = 40 * 1024 * 1024

F32 = jnp.float32
BF16 = jnp.bfloat16

ANY = pl.BlockSpec(memory_space=pl.ANY)
SMEM = pl.BlockSpec(memory_space=pltpu.SMEM)
VMEM = pl.BlockSpec(memory_space=pltpu.VMEM)


def params():
    return pltpu.CompilerParams(vmem_limit_bytes=VMEM_LIMIT)


def cost(flops, nbytes):
    return pl.CostEstimate(flops=int(flops), bytes_accessed=int(nbytes), transcendentals=0)


def shifted(n, d):
    return [(s, (s + d) % n) for s in range(n)]


def pick_kernel(start, rows, index_ref, blocks_ref, *rest):
    outs, sems = rest[:-1], rest[-1]
    copies = []
    for d, out in enumerate(outs):
        for k in range(CAP):
            copies.append(
                pltpu.make_async_copy(
                    blocks_ref.at[index_ref[d, k], pl.ds(start, rows)],
                    out.at[k],
                    sems.at[d * CAP + k],
                )
            )
    for c in copies:
        c.start()
    for c in copies:
        c.wait()


def pick_blocks(index, blocks, start, rows):
    count = index.shape[0]
    virt = blocks.shape[2]
    shape = jax.ShapeDtypeStruct((CAP, rows, virt), BF16)
    return pl.pallas_call(
        functools.partial(pick_kernel, start, rows),
        out_shape=[shape] * count,
        in_specs=[SMEM, ANY],
        out_specs=[ANY] * count,
        scratch_shapes=[pltpu.SemaphoreType.DMA((count * CAP,))],
        compiler_params=params(),
        cost_estimate=cost(0, 2 * count * CAP * rows * virt * 2),
        name="pick_blocks",
    )(index, blocks)


def load_slots(own_ref, blocks_ref, arrived, held, sems, start, offset, rows):
    copies = []
    for k in range(CAP):
        copies.append(
            pltpu.make_async_copy(
                blocks_ref.at[own_ref[k], pl.ds(start, rows)], held.at[k], sems.at[k]
            )
        )
    for d, ref in enumerate(arrived):
        for k in range(CAP):
            s = (d + 1) * CAP + k
            copies.append(
                pltpu.make_async_copy(ref.at[k, pl.ds(offset, rows)], held.at[s], sems.at[s])
            )
    for c in copies:
        c.start()
    return copies


def exchange_kernel(start, rows, first, n, slot_ref, own_ref, blocks_ref, *rest):
    arrived = rest[: n - 1]
    rest = rest[n - 1 :]
    if not first:
        before_ref, rest = rest[0], rest[1:]
    out_ref, held, sems = rest
    for c in load_slots(own_ref, blocks_ref, arrived, held, sems, start, 0, rows):
        c.wait()

    def step(p, carry):
        product = lax.dot_general(
            held[slot_ref[2 * p]],
            held[slot_ref[2 * p + 1]],
            (((0,), (0,)), ((), ())),
            preferred_element_type=F32,
        )
        if not first:
            product = product + before_ref[p]
        out_ref[p] = product.astype(out_ref.dtype)
        return carry

    lax.fori_loop(0, out_ref.shape[0], step, 0)


def exchange_chunk(slots, own, blocks, arrived, before, start, rows, last):
    n = len(arrived) + 1
    pairs = slots.shape[0] // 2
    virt = blocks.shape[2]
    first = before is None
    return pl.pallas_call(
        functools.partial(exchange_kernel, start, rows, first, n),
        out_shape=jax.ShapeDtypeStruct((pairs, virt, virt), BF16 if last else F32),
        in_specs=[SMEM, SMEM, ANY] + [ANY] * (n - 1) + ([] if first else [VMEM]),
        out_specs=VMEM,
        scratch_shapes=[
            pltpu.VMEM((n * CAP, rows, virt), BF16),
            pltpu.SemaphoreType.DMA((n * CAP,)),
        ],
        compiler_params=params(),
        cost_estimate=cost(
            2 * pairs * rows * virt * virt, n * CAP * rows * virt * 2 + pairs * virt * virt * 6
        ),
        name="exchange_chunk",
    )(slots, own, blocks, *arrived, *([] if first else [before]))


def amplitude_kernel(parts, energy_ref, ends_ref, size_ref, fock_ref, *rest):
    ints = rest[:parts]
    amp_ref, weight_ref = rest[parts:]
    p = pl.program_id(0)
    virt = fock_ref.shape[-1]
    occ = energy_ref[ends_ref[2 * p]] + energy_ref[ends_ref[2 * p + 1]]
    size = size_ref[p]
    fock = fock_ref[0]
    row = lax.broadcasted_iota(jnp.int32, (virt, virt), 0)
    col = lax.broadcasted_iota(jnp.int32, (virt, virt), 1)
    on_diagonal = row == col
    diagonal = jnp.where(on_diagonal, fock, 0.0)
    denominator = (
        jnp.sum(diagonal, axis=1, keepdims=True) + jnp.sum(diagonal, axis=0, keepdims=True) - occ
    )
    inverse = jnp.where((row < size) & (col < size), 1.0 / denominator, 0.0)
    total = ints[0][0].astype(F32)
    for ref in ints[1:]:
        total = total + ref[0].astype(F32)
    current = -total * inverse
    off = jnp.where(on_diagonal, 0.0, fock)
    off_high = off.astype(BF16)
    cur_high = current.astype(BF16)
    change = jnp.dot(off_high, cur_high, preferred_element_type=F32) + jnp.dot(
        cur_high, off_high, preferred_element_type=F32
    )
    amp = (current - change * inverse).astype(BF16)
    amp_ref[0] = amp
    wide = amp.astype(F32)
    flipped = wide.T
    weight_ref[0] = (2.0 * flipped - wide).astype(BF16)
    weight_ref[1] = (2.0 * wide - flipped).astype(BF16)


def amplitude_step(energies, ends, sizes, fock, ints):
    pairs, virt, _ = fock.shape
    block = pl.BlockSpec((1, virt, virt), lambda p: (p, 0, 0))
    return pl.pallas_call(
        functools.partial(amplitude_kernel, len(ints)),
        grid=(pairs,),
        out_shape=[
            jax.ShapeDtypeStruct((pairs, virt, virt), BF16),
            jax.ShapeDtypeStruct((2 * pairs, virt, virt), BF16),
        ],
        in_specs=[SMEM, SMEM, SMEM, block] + [block] * len(ints),
        out_specs=[block, pl.BlockSpec((2, virt, virt), lambda p: (p, 0, 0))],
        compiler_params=params(),
        cost_estimate=cost(4 * pairs * virt**3, pairs * virt * virt * 14),
        name="amplitude_step",
    )(energies, ends, sizes, fock, *ints)


def gradient_kernel(start, offset, rows, n, slot_ref, own_ref, weight_ref, blocks_ref, *rest):
    arrived = rest[: n - 1]
    outs = rest[n - 1 : 2 * n - 1]
    held, sums, sems = rest[2 * n - 1 :]
    copies = load_slots(own_ref, blocks_ref, arrived, held, sems, start, offset, rows)
    sums[...] = jnp.zeros_like(sums)
    for c in copies:
        c.wait()

    def step(p, carry):
        left = slot_ref[2 * p]
        right = slot_ref[2 * p + 1]
        sums[left] += jnp.dot(held[right], weight_ref[2 * p], preferred_element_type=F32)
        sums[right] += jnp.dot(held[left], weight_ref[2 * p + 1], preferred_element_type=F32)
        return carry

    lax.fori_loop(0, weight_ref.shape[0] // 2, step, 0)
    for d, out in enumerate(outs):
        for k in range(CAP):
            out[k] = sums[d * CAP + k].astype(BF16)


def gradient_chunk(slots, own, weights, blocks, arrived, start, offset, rows):
    n = len(arrived) + 1
    ends = slots.shape[0]
    virt = blocks.shape[2]
    return pl.pallas_call(
        functools.partial(gradient_kernel, start, offset, rows, n),
        out_shape=[jax.ShapeDtypeStruct((CAP, rows, virt), BF16)] * n,
        in_specs=[SMEM, SMEM, VMEM, ANY] + [ANY] * (n - 1),
        out_specs=[VMEM] * n,
        scratch_shapes=[
            pltpu.VMEM((n * CAP, rows, virt), BF16),
            pltpu.VMEM((n * CAP, rows, virt), F32),
            pltpu.SemaphoreType.DMA((n * CAP,)),
        ],
        compiler_params=params(),
        cost_estimate=cost(
            2 * ends * rows * virt * virt, 4 * n * CAP * rows * virt + ends * virt * virt * 2
        ),
        name="gradient_chunk",
    )(slots, own, weights, blocks, *arrived)


def collect_kernel(count, index_ref, *rest):
    terms = rest[:count]
    out_ref = rest[-1]
    out_ref[...] = jnp.zeros_like(out_ref)
    for d, ref in enumerate(terms):
        for k in range(CAP):
            g = index_ref[d, k]
            out_ref[g] += ref[k].astype(F32)


def collect_chunk(index, terms, before, local_orbs, fit_rows, start, rows):
    virt = terms[0].shape[2]
    count = len(terms)
    more = [] if before is None else [before]
    at = start // rows
    return pl.pallas_call(
        functools.partial(collect_kernel, count),
        grid=(1,),
        out_shape=jax.ShapeDtypeStruct((local_orbs, fit_rows, virt), F32),
        in_specs=[SMEM]
        + [pl.BlockSpec((CAP, rows, virt), lambda i: (0, 0, 0))] * count
        + [ANY] * len(more),
        out_specs=pl.BlockSpec((local_orbs, rows, virt), lambda i: (0, at, 0)),
        input_output_aliases={} if before is None else {1 + count: 0},
        compiler_params=params(),
        cost_estimate=cost(0, (count * CAP * 2 + local_orbs * 4) * rows * virt),
        name="collect_chunk",
    )(index, *terms, *more)


def per_device(blocks, occ_energy, pair_list, pno_sizes, fock_virt):
    n = lax.axis_size("orb")
    n_fit = lax.axis_size("fit")
    n_rep = lax.axis_size("rep")
    local_orbs, fit_rows, virt = blocks.shape
    total_orbs = local_orbs * n
    me = lax.axis_index("orb")

    endpoints = pair_list.reshape(-1)
    relative = (endpoints - me * local_orbs) % total_orbs
    named = jnp.any(
        relative[:, None] == jnp.arange(total_orbs, dtype=jnp.int32)[None, :], axis=0
    ).reshape(n, local_orbs)
    table = named.astype(jnp.int32)
    position = jnp.cumsum(table, axis=1) - 1
    columns = jnp.arange(CAP, dtype=jnp.int32)
    locals_ = jnp.arange(local_orbs, dtype=jnp.int32)
    matches = table[:, :, None] * (position[:, :, None] == columns[None, None, :])
    wanted = jnp.sum(matches * locals_[None, :, None], axis=1)
    end_hot = relative[:, None] == jnp.arange(total_orbs, dtype=jnp.int32)[None, :]
    slots = (relative // local_orbs) * CAP + jnp.sum(
        jnp.where(end_hot, position.reshape(1, -1), 0), axis=1
    )
    slots = slots.astype(jnp.int32)

    energies_here = occ_energy.astype(F32)
    got = {}
    for d in range(1, n):
        note = jnp.concatenate([wanted[d].astype(F32), energies_here])
        got[d] = lax.ppermute(note, "orb", shifted(n, d))
    asked = jnp.stack(
        [wanted[0]] + [got[d][:CAP].astype(jnp.int32) for d in range(1, n)]
    )
    energies = jnp.concatenate([energies_here] + [got[n - d][CAP:] for d in range(1, n)])

    forward_chunks = FORWARD_CHUNKS
    rows = fit_rows // forward_chunks
    own = wanted[0]
    arrived = []
    for c in range(forward_chunks):
        picked = pick_blocks(asked[1:], blocks, c * rows, rows)
        arrived.append(
            [lax.ppermute(picked[d - 1], "orb", shifted(n, n - d)) for d in range(1, n)]
        )
    ints = None
    for c in range(forward_chunks):
        ints = exchange_chunk(
            slots, own, blocks, arrived[c], ints, c * rows, rows, c == forward_chunks - 1
        )
    if n_fit == 2:
        parts = [ints, lax.ppermute(ints, "fit", shifted(2, 1))]
    elif n_fit > 1:
        every = lax.all_gather(ints, "fit")
        parts = [every[i] for i in range(n_fit)]
    else:
        parts = [ints]
    amplitudes, weights = amplitude_step(energies, relative, pno_sizes, fock_virt, parts)

    swap = shifted(n_rep, 1)
    both = [asked, lax.ppermute(asked.astype(F32), "rep", swap).astype(jnp.int32)]
    index = jnp.concatenate(both)
    back_rows = fit_rows // BACK_CHUNKS
    returned = []
    for c in range(BACK_CHUNKS):
        start = c * back_rows
        sums = gradient_chunk(
            slots, own, weights, blocks, arrived[start // rows], start, start % rows, back_rows
        )
        returned.append(
            [sums[0]] + [lax.ppermute(sums[d], "orb", shifted(n, d)) for d in range(1, n)]
        )
    grads = None
    for c in range(BACK_CHUNKS):
        other = [lax.ppermute(x, "rep", swap) for x in returned[c]]
        grads = collect_chunk(
            index, returned[c] + other, grads, local_orbs, fit_rows, c * back_rows, back_rows
        )
    return amplitudes, grads


def solution(mesh):
    placed = (
        P(("groups", "orb"), "fit", None),
        P(("groups", "orb")),
        P(("groups", "orb", "rep"), None),
        P(("groups", "orb", "rep")),
        P(("groups", "orb", "rep"), None, None),
    )
    return jax.shard_map(
        per_device,
        mesh=mesh,
        in_specs=placed,
        out_specs=(P(("groups", "orb", "rep"), None, None), P(("groups", "orb"), "fit", None)),
        check_vma=False,
    )
```

```python
import functools

import jax
import jax.numpy as jnp
from jax import lax
from jax.experimental import pallas as pl
from jax.experimental.pallas import tpu as pltpu
from jax.sharding import PartitionSpec as P

CAP = 2
FORWARD_CHUNKS = 4
BACK_CHUNKS = 4
VMEM_LIMIT = 40 * 1024 * 1024

F32 = jnp.float32
BF16 = jnp.bfloat16

ANY = pl.BlockSpec(memory_space=pl.ANY)
SMEM = pl.BlockSpec(memory_space=pltpu.SMEM)
VMEM = pl.BlockSpec(memory_space=pltpu.VMEM)


def params():
    return pltpu.CompilerParams(vmem_limit_bytes=VMEM_LIMIT)


def cost(flops, nbytes):
    return pl.CostEstimate(flops=int(flops), bytes_accessed=int(nbytes), transcendentals=0)


def shifted(n, d):
    return [(s, (s + d) % n) for s in range(n)]


def pick_kernel(start, rows, index_ref, blocks_ref, *rest):
    outs, sems = rest[:-1], rest[-1]
    copies = []
    for d, out in enumerate(outs):
        for k in range(CAP):
            copies.append(
                pltpu.make_async_copy(
                    blocks_ref.at[index_ref[d, k], pl.ds(start, rows)],
                    out.at[k],
                    sems.at[d * CAP + k],
                )
            )
    for c in copies:
        c.start()
    for c in copies:
        c.wait()


def pick_blocks(index, blocks, start, rows):
    count = index.shape[0]
    virt = blocks.shape[2]
    shape = jax.ShapeDtypeStruct((CAP, rows, virt), BF16)
    return pl.pallas_call(
        functools.partial(pick_kernel, start, rows),
        out_shape=[shape] * count,
        in_specs=[SMEM, ANY],
        out_specs=[ANY] * count,
        scratch_shapes=[pltpu.SemaphoreType.DMA((count * CAP,))],
        compiler_params=params(),
        cost_estimate=cost(0, 2 * count * CAP * rows * virt * 2),
        name="pick_blocks",
    )(index, blocks)


def load_slots(own_ref, blocks_ref, arrived, held, sems, start, offset, rows):
    copies = []
    for k in range(CAP):
        copies.append(
            pltpu.make_async_copy(
                blocks_ref.at[own_ref[k], pl.ds(start, rows)], held.at[k], sems.at[k]
            )
        )
    for d, ref in enumerate(arrived):
        for k in range(CAP):
            s = (d + 1) * CAP + k
            copies.append(
                pltpu.make_async_copy(ref.at[k, pl.ds(offset, rows)], held.at[s], sems.at[s])
            )
    for c in copies:
        c.start()
    return copies


def exchange_kernel(start, rows, first, n, slot_ref, own_ref, blocks_ref, *rest):
    arrived = rest[: n - 1]
    rest = rest[n - 1 :]
    if not first:
        before_ref, rest = rest[0], rest[1:]
    out_ref, held, sems = rest
    for c in load_slots(own_ref, blocks_ref, arrived, held, sems, start, 0, rows):
        c.wait()

    def step(p, carry):
        product = lax.dot_general(
            held[slot_ref[2 * p]],
            held[slot_ref[2 * p + 1]],
            (((0,), (0,)), ((), ())),
            preferred_element_type=F32,
        )
        if not first:
            product = product + before_ref[p]
        out_ref[p] = product.astype(out_ref.dtype)
        return carry

    lax.fori_loop(0, out_ref.shape[0], step, 0)


def exchange_chunk(slots, own, blocks, arrived, before, start, rows, last):
    n = len(arrived) + 1
    pairs = slots.shape[0] // 2
    virt = blocks.shape[2]
    first = before is None
    return pl.pallas_call(
        functools.partial(exchange_kernel, start, rows, first, n),
        out_shape=jax.ShapeDtypeStruct((pairs, virt, virt), BF16 if last else F32),
        in_specs=[SMEM, SMEM, ANY] + [ANY] * (n - 1) + ([] if first else [VMEM]),
        out_specs=VMEM,
        scratch_shapes=[
            pltpu.VMEM((n * CAP, rows, virt), BF16),
            pltpu.SemaphoreType.DMA((n * CAP,)),
        ],
        compiler_params=params(),
        cost_estimate=cost(
            2 * pairs * rows * virt * virt, n * CAP * rows * virt * 2 + pairs * virt * virt * 6
        ),
        name="exchange_chunk",
    )(slots, own, blocks, *arrived, *([] if first else [before]))


def amplitude_kernel(parts, energy_ref, ends_ref, size_ref, fock_ref, *rest):
    ints = rest[:parts]
    amp_ref, weight_ref = rest[parts:]
    p = pl.program_id(0)
    virt = fock_ref.shape[-1]
    occ = energy_ref[ends_ref[2 * p]] + energy_ref[ends_ref[2 * p + 1]]
    size = size_ref[p]
    fock = fock_ref[0]
    row = lax.broadcasted_iota(jnp.int32, (virt, virt), 0)
    col = lax.broadcasted_iota(jnp.int32, (virt, virt), 1)
    on_diagonal = row == col
    diagonal = jnp.where(on_diagonal, fock, 0.0)
    denominator = (
        jnp.sum(diagonal, axis=1, keepdims=True) + jnp.sum(diagonal, axis=0, keepdims=True) - occ
    )
    inverse = jnp.where((row < size) & (col < size), 1.0 / denominator, 0.0)
    total = ints[0][0].astype(F32)
    for ref in ints[1:]:
        total = total + ref[0].astype(F32)
    current = -total * inverse
    off = jnp.where(on_diagonal, 0.0, fock)
    off_high = off.astype(BF16)
    cur_high = current.astype(BF16)
    change = jnp.dot(off_high, cur_high, preferred_element_type=F32) + jnp.dot(
        cur_high, off_high, preferred_element_type=F32
    )
    amp = (current - change * inverse).astype(BF16)
    amp_ref[0] = amp
    wide = amp.astype(F32)
    flipped = wide.T
    weight_ref[0] = (2.0 * flipped - wide).astype(BF16)
    weight_ref[1] = (2.0 * wide - flipped).astype(BF16)


def amplitude_step(energies, ends, sizes, fock, ints):
    pairs, virt, _ = fock.shape
    block = pl.BlockSpec((1, virt, virt), lambda p: (p, 0, 0))
    return pl.pallas_call(
        functools.partial(amplitude_kernel, len(ints)),
        grid=(pairs,),
        out_shape=[
            jax.ShapeDtypeStruct((pairs, virt, virt), BF16),
            jax.ShapeDtypeStruct((2 * pairs, virt, virt), BF16),
        ],
        in_specs=[SMEM, SMEM, SMEM, block] + [block] * len(ints),
        out_specs=[block, pl.BlockSpec((2, virt, virt), lambda p: (p, 0, 0))],
        compiler_params=params(),
        cost_estimate=cost(4 * pairs * virt**3, pairs * virt * virt * 14),
        name="amplitude_step",
    )(energies, ends, sizes, fock, *ints)


def gradient_kernel(start, offset, rows, n, slot_ref, own_ref, weight_ref, blocks_ref, *rest):
    arrived = rest[: n - 1]
    outs = rest[n - 1 : 2 * n - 1]
    held, sums, sems = rest[2 * n - 1 :]
    copies = load_slots(own_ref, blocks_ref, arrived, held, sems, start, offset, rows)
    sums[...] = jnp.zeros_like(sums)
    for c in copies:
        c.wait()

    def step(p, carry):
        left = slot_ref[2 * p]
        right = slot_ref[2 * p + 1]
        sums[left] += jnp.dot(held[right], weight_ref[2 * p], preferred_element_type=F32)
        sums[right] += jnp.dot(held[left], weight_ref[2 * p + 1], preferred_element_type=F32)
        return carry

    lax.fori_loop(0, weight_ref.shape[0] // 2, step, 0)
    for d, out in enumerate(outs):
        for k in range(CAP):
            out[k] = sums[d * CAP + k].astype(BF16)


def gradient_chunk(slots, own, weights, blocks, arrived, start, offset, rows):
    n = len(arrived) + 1
    ends = slots.shape[0]
    virt = blocks.shape[2]
    return pl.pallas_call(
        functools.partial(gradient_kernel, start, offset, rows, n),
        out_shape=[jax.ShapeDtypeStruct((CAP, rows, virt), BF16)] * n,
        in_specs=[SMEM, SMEM, VMEM, ANY] + [ANY] * (n - 1),
        out_specs=[VMEM] * n,
        scratch_shapes=[
            pltpu.VMEM((n * CAP, rows, virt), BF16),
            pltpu.VMEM((n * CAP, rows, virt), F32),
            pltpu.SemaphoreType.DMA((n * CAP,)),
        ],
        compiler_params=params(),
        cost_estimate=cost(
            2 * ends * rows * virt * virt, 4 * n * CAP * rows * virt + ends * virt * virt * 2
        ),
        name="gradient_chunk",
    )(slots, own, weights, blocks, *arrived)


def collect_kernel(count, index_ref, *rest):
    terms = rest[:count]
    out_ref, sums = rest[count:]
    sums[...] = jnp.zeros_like(sums)
    for d, ref in enumerate(terms):
        for k in range(CAP):
            g = index_ref[d, k]
            sums[g] += ref[k].astype(F32)
    out_ref[...] = sums[...].astype(BF16)


def collect_chunk(index, terms, local_orbs):
    _, rows, virt = terms[0].shape
    count = len(terms)
    return pl.pallas_call(
        functools.partial(collect_kernel, count),
        out_shape=jax.ShapeDtypeStruct((local_orbs, rows, virt), BF16),
        in_specs=[SMEM] + [VMEM] * count,
        out_specs=VMEM,
        scratch_shapes=[pltpu.VMEM((local_orbs, rows, virt), F32)],
        compiler_params=params(),
        cost_estimate=cost(0, (count * CAP + local_orbs) * 2 * rows * virt),
        name="collect_chunk",
    )(index, *terms)


def add_kernel(mine_ref, other_ref, *rest):
    rest[-1][...] = mine_ref[...].astype(F32) + other_ref[...].astype(F32)


def add_chunk(mine, other, before, fit_rows, start):
    local_orbs, rows, virt = mine.shape
    step = min(rows, 64)
    at = start // step
    more = [] if before is None else [before]
    source = pl.BlockSpec((local_orbs, step, virt), lambda i: (0, i, 0))
    return pl.pallas_call(
        add_kernel,
        grid=(rows // step,),
        out_shape=jax.ShapeDtypeStruct((local_orbs, fit_rows, virt), F32),
        in_specs=[source, source] + [ANY] * len(more),
        out_specs=pl.BlockSpec((local_orbs, step, virt), lambda i: (0, at + i, 0)),
        input_output_aliases={} if before is None else {2: 0},
        compiler_params=params(),
        cost_estimate=cost(0, 8 * local_orbs * rows * virt),
        name="add_chunk",
    )(mine, other, *more)


def per_device(blocks, occ_energy, pair_list, pno_sizes, fock_virt):
    n = lax.axis_size("orb")
    n_fit = lax.axis_size("fit")
    n_rep = lax.axis_size("rep")
    local_orbs, fit_rows, virt = blocks.shape
    total_orbs = local_orbs * n
    me = lax.axis_index("orb")

    endpoints = pair_list.reshape(-1)
    relative = (endpoints - me * local_orbs) % total_orbs
    named = jnp.any(
        relative[:, None] == jnp.arange(total_orbs, dtype=jnp.int32)[None, :], axis=0
    ).reshape(n, local_orbs)
    table = named.astype(jnp.int32)
    position = jnp.cumsum(table, axis=1) - 1
    columns = jnp.arange(CAP, dtype=jnp.int32)
    locals_ = jnp.arange(local_orbs, dtype=jnp.int32)
    matches = table[:, :, None] * (position[:, :, None] == columns[None, None, :])
    wanted = jnp.sum(matches * locals_[None, :, None], axis=1)
    end_hot = relative[:, None] == jnp.arange(total_orbs, dtype=jnp.int32)[None, :]
    slots = (relative // local_orbs) * CAP + jnp.sum(
        jnp.where(end_hot, position.reshape(1, -1), 0), axis=1
    )
    slots = slots.astype(jnp.int32)

    energies_here = occ_energy.astype(F32)
    got = {}
    for d in range(1, n):
        note = jnp.concatenate([wanted[d].astype(F32), energies_here])
        got[d] = lax.ppermute(note, "orb", shifted(n, d))
    asked = jnp.stack(
        [wanted[0]] + [got[d][:CAP].astype(jnp.int32) for d in range(1, n)]
    )
    energies = jnp.concatenate([energies_here] + [got[n - d][CAP:] for d in range(1, n)])

    forward_chunks = FORWARD_CHUNKS
    rows = fit_rows // forward_chunks
    own = wanted[0]
    arrived = []
    for c in range(forward_chunks):
        picked = pick_blocks(asked[1:], blocks, c * rows, rows)
        arrived.append(
            [lax.ppermute(picked[d - 1], "orb", shifted(n, n - d)) for d in range(1, n)]
        )
    ints = None
    for c in range(forward_chunks):
        ints = exchange_chunk(
            slots, own, blocks, arrived[c], ints, c * rows, rows, c == forward_chunks - 1
        )
    if n_fit == 2:
        parts = [ints, lax.ppermute(ints, "fit", shifted(2, 1))]
    elif n_fit > 1:
        every = lax.all_gather(ints, "fit")
        parts = [every[i] for i in range(n_fit)]
    else:
        parts = [ints]
    amplitudes, weights = amplitude_step(energies, relative, pno_sizes, fock_virt, parts)

    swap = shifted(n_rep, 1)
    back_rows = fit_rows // BACK_CHUNKS
    returned = []
    for c in range(BACK_CHUNKS):
        start = c * back_rows
        sums = gradient_chunk(
            slots, own, weights, blocks, arrived[start // rows], start, start % rows, back_rows
        )
        returned.append(
            [sums[0]] + [lax.ppermute(sums[d], "orb", shifted(n, d)) for d in range(1, n)]
        )
    grads = None
    for c in range(BACK_CHUNKS):
        mine = collect_chunk(asked, returned[c], local_orbs)
        other = lax.ppermute(mine, "rep", swap)
        grads = add_chunk(mine, other, grads, fit_rows, c * back_rows)
    return amplitudes, grads


def solution(mesh):
    placed = (
        P(("groups", "orb"), "fit", None),
        P(("groups", "orb")),
        P(("groups", "orb", "rep"), None),
        P(("groups", "orb", "rep")),
        P(("groups", "orb", "rep"), None, None),
    )
    return jax.shard_map(
        per_device,
        mesh=mesh,
        in_specs=placed,
        out_specs=(P(("groups", "orb", "rep"), None, None), P(("groups", "orb"), "fit", None)),
        check_vma=False,
    )
```

```python
import functools
from typing import NamedTuple

import jax
import jax.numpy as jnp
from jax import lax
from jax.experimental import pallas as pl
from jax.experimental.pallas import tpu as pltpu
from jax.sharding import PartitionSpec as P

CAP = 2
FORWARD_ROWS = (21, 16, 12, 9, 6)
BACK_ROWS = (14, 14, 15, 15)
BACK_GROUPS = (2, 3, 4, 5)
SETTLE_WEIGHT = 50
MERGE_WEIGHT = 50
EXCHANGE_WEIGHT = 50
VMEM_LIMIT = 40 * 1024 * 1024

F32 = jnp.float32
BF16 = jnp.bfloat16

ANY = pl.BlockSpec(memory_space=pl.ANY)
SMEM = pl.BlockSpec(memory_space=pltpu.SMEM)
VMEM = pl.BlockSpec(memory_space=pltpu.VMEM)


def params():
    return pltpu.CompilerParams(vmem_limit_bytes=VMEM_LIMIT)


def cost(flops, nbytes):
    return pl.CostEstimate(flops=int(flops), bytes_accessed=int(nbytes), transcendentals=0)


def weighed(times, flops, nbytes):
    return cost(times * flops, times * nbytes)


def shifted(n, d):
    return [(s, (s + d) % n) for s in range(n)]


def pick_kernel(start, rows, waits, index_ref, blocks_ref, *rest):
    outs, sems = rest[waits:-1], rest[-1]
    copies = []
    for d, out in enumerate(outs):
        for k in range(CAP):
            copies.append(
                pltpu.make_async_copy(
                    blocks_ref.at[index_ref[d, k], pl.ds(start, rows)],
                    out.at[k],
                    sems.at[d * CAP + k],
                )
            )
    for c in copies:
        c.start()
    for c in copies:
        c.wait()


def pick_blocks(index, blocks, start, rows, after=()):
    count = index.shape[0]
    virt = blocks.shape[2]
    shape = jax.ShapeDtypeStruct((CAP, rows, virt), BF16)
    return pl.pallas_call(
        functools.partial(pick_kernel, start, rows, len(after)),
        out_shape=[shape] * count,
        in_specs=[SMEM, ANY] + [ANY] * len(after),
        out_specs=[ANY] * count,
        scratch_shapes=[pltpu.SemaphoreType.DMA((count * CAP,))],
        compiler_params=params(),
        cost_estimate=cost(0, 2 * count * CAP * rows * virt * 2),
        name="pick_blocks",
    )(index, blocks, *after)


def merge_kernel(count, *refs):
    sources, out, sems = refs[:count], refs[-2], refs[-1]
    copies = [
        pltpu.make_async_copy(ref, out.at[pl.ds(d * CAP, CAP)], sems.at[d])
        for d, ref in enumerate(sources)
    ]
    for c in copies:
        c.start()
    for c in copies:
        c.wait()


def merge_chunk(arrived, after=()):
    count = len(arrived)
    _, rows, virt = arrived[0].shape
    return pl.pallas_call(
        functools.partial(merge_kernel, count),
        out_shape=jax.ShapeDtypeStruct((count * CAP, rows, virt), BF16),
        in_specs=[ANY] * (count + len(after)),
        out_specs=ANY,
        scratch_shapes=[pltpu.SemaphoreType.DMA((count,))],
        compiler_params=params(),
        cost_estimate=weighed(MERGE_WEIGHT, 0, 4 * count * CAP * rows * virt),
        name="merge_chunk",
    )(*arrived, *after)


class Rows(NamedTuple):
    start: int
    count: int


def load_all(fit_ref, chunks, mine, merged, held, sems):
    n_fit = len(mine)
    total = sum(c.count for c in chunks)
    copies = []
    for f in range(n_fit):
        place = lax.rem(fit_ref[0] + (n_fit - f), n_fit)
        at = 0
        for i, c in enumerate(chunks):
            rows = pl.ds(pl.multiple_of(place * total + at, 16), c.count)
            copies.append(
                pltpu.make_async_copy(
                    mine[f].at[:, pl.ds(c.start, c.count)],
                    held.at[pl.ds(0, CAP), rows],
                    sems.at[len(copies)],
                )
            )
            copies.append(
                pltpu.make_async_copy(
                    merged[i][f],
                    held.at[pl.ds(CAP, held.shape[0] - CAP), rows],
                    sems.at[len(copies)],
                )
            )
            at += c.count
    for c in copies:
        c.start()
    return copies


def cross(left, right):
    return lax.dot_general(left, right, (((0,), (0,)), ((), ())), preferred_element_type=F32)


def split_refs(rest, n_fit, chunks):
    mine, rest = rest[:n_fit], rest[n_fit:]
    merged = []
    for _ in chunks:
        merged.append(rest[:n_fit])
        rest = rest[n_fit:]
    return mine, merged, rest


def exchange_kernel(chunks, n_fit, first, waits, slot_ref, fit_ref, *rest):
    mine, merged, rest = split_refs(rest[waits:], n_fit, chunks)
    if not first:
        before_ref, rest = rest[0], rest[1:]
    out_ref, held, sems = rest
    for c in load_all(fit_ref, chunks, mine, merged, held, sems):
        c.wait()

    def step(p, carry):
        product = cross(held[slot_ref[2 * p]], held[slot_ref[2 * p + 1]])
        if not first:
            product = before_ref[p] + product
        out_ref[p] = product
        return carry

    lax.fori_loop(0, out_ref.shape[0], step, 0)


def exchange_chunks(slots, fit, chunks, mine, merged, before, after=()):
    n_fit = len(mine)
    pairs = slots.shape[0] // 2
    virt = mine[0].shape[2]
    all_slots = CAP + merged[0][0].shape[0]
    rows = sum(c.count for c in chunks) * n_fit
    first = before is None
    return pl.pallas_call(
        functools.partial(exchange_kernel, chunks, n_fit, first, len(after)),
        out_shape=jax.ShapeDtypeStruct((pairs, virt, virt), F32),
        in_specs=[SMEM, SMEM]
        + [ANY] * (len(after) + n_fit * (1 + len(chunks)))
        + ([] if first else [VMEM]),
        out_specs=VMEM,
        scratch_shapes=[
            pltpu.VMEM((all_slots, rows, virt), BF16),
            pltpu.SemaphoreType.DMA((2 * n_fit * len(chunks),)),
        ],
        compiler_params=params(),
        cost_estimate=weighed(EXCHANGE_WEIGHT,
            2 * pairs * rows * virt * virt, all_slots * rows * virt * 2 + pairs * virt * virt * 8
        ),
        name="exchange_chunks",
    )(slots, fit, *after, *mine, *[x for m in merged for x in m], *([] if first else [before]))


def prepare_kernel(energy_ref, ends_ref, size_ref, fock_ref, inverse_ref, off_ref):
    p = pl.program_id(0)
    virt = fock_ref.shape[-1]
    occ = energy_ref[ends_ref[2 * p]] + energy_ref[ends_ref[2 * p + 1]]
    size = size_ref[p]
    fock = fock_ref[0]
    row = lax.broadcasted_iota(jnp.int32, (virt, virt), 0)
    col = lax.broadcasted_iota(jnp.int32, (virt, virt), 1)
    on_diagonal = row == col
    diagonal = jnp.where(on_diagonal, fock, 0.0)
    denominator = (
        jnp.sum(diagonal, axis=1, keepdims=True) + jnp.sum(diagonal, axis=0, keepdims=True) - occ
    )
    inverse_ref[0] = jnp.where((row < size) & (col < size), 1.0 / denominator, 0.0)
    off_ref[0] = jnp.where(on_diagonal, 0.0, fock).astype(BF16)


def prepare_pairs(energies, ends, sizes, fock):
    pairs, virt, _ = fock.shape
    block = pl.BlockSpec((1, virt, virt), lambda p: (p, 0, 0))
    return pl.pallas_call(
        prepare_kernel,
        grid=(pairs,),
        out_shape=[
            jax.ShapeDtypeStruct((pairs, virt, virt), F32),
            jax.ShapeDtypeStruct((pairs, virt, virt), BF16),
        ],
        in_specs=[SMEM, SMEM, SMEM, block],
        out_specs=[block, block],
        compiler_params=params(),
        cost_estimate=cost(10 * pairs * virt * virt, pairs * virt * virt * 10),
        name="prepare_pairs",
    )(energies, ends, sizes, fock)


def add_gradients(slot_ref, weight_ref, block_of, sums, outs):
    sums[...] = jnp.zeros_like(sums)

    def step(p, carry):
        left = slot_ref[2 * p]
        right = slot_ref[2 * p + 1]
        sums[left] += jnp.dot(block_of(right), weight_ref[2 * p], preferred_element_type=F32)
        sums[right] += jnp.dot(block_of(left), weight_ref[2 * p + 1], preferred_element_type=F32)
        return carry

    lax.fori_loop(0, weight_ref.shape[0] // 2, step, 0)
    for d, out in enumerate(outs):
        for k in range(CAP):
            out[k] = sums[d * CAP + k].astype(BF16)


def middle_kernel(chunk, n, n_fit, slot_ref, fit_ref, *rest):
    mine, merged, rest = split_refs(rest, n_fit, [chunk])
    before_ref, inverse_ref, off_ref, amp_ref, weight_ref = rest[:5]
    outs = rest[5 : 5 + n]
    held, sums, sems = rest[5 + n :]
    for c in load_all(fit_ref, [chunk], mine, merged, held, sems):
        c.wait()

    def step(p, carry):
        total = before_ref[p] + cross(held[slot_ref[2 * p]], held[slot_ref[2 * p + 1]])
        inverse = inverse_ref[p]
        off = off_ref[p]
        current = -total * inverse
        rounded = current.astype(BF16)
        change = jnp.dot(off, rounded, preferred_element_type=F32) + jnp.dot(
            rounded, off, preferred_element_type=F32
        )
        amp = (current - change * inverse).astype(BF16)
        amp_ref[p] = amp
        wide = amp.astype(F32)
        flipped = wide.T
        weight_ref[2 * p] = (2.0 * flipped - wide).astype(BF16)
        weight_ref[2 * p + 1] = (2.0 * wide - flipped).astype(BF16)
        return carry

    lax.fori_loop(0, amp_ref.shape[0], step, 0, unroll=2)
    here = pl.ds(pl.multiple_of(fit_ref[0] * chunk.count, 16), chunk.count)
    add_gradients(slot_ref, weight_ref, lambda s: held[s, here], sums, outs)


def middle_step(slots, fit, chunk, mine, merged, before, inverse, off):
    n_fit = len(mine)
    pairs, virt, _ = before.shape
    all_slots = CAP + merged[0].shape[0]
    n = all_slots // CAP
    return pl.pallas_call(
        functools.partial(middle_kernel, chunk, n, n_fit),
        out_shape=[
            jax.ShapeDtypeStruct((pairs, virt, virt), BF16),
            jax.ShapeDtypeStruct((2 * pairs, virt, virt), BF16),
        ]
        + [jax.ShapeDtypeStruct((CAP, chunk.count, virt), BF16)] * n,
        in_specs=[SMEM, SMEM] + [ANY] * (2 * n_fit) + [VMEM] * 3,
        out_specs=[VMEM] * (2 + n),
        scratch_shapes=[
            pltpu.VMEM((all_slots, n_fit * chunk.count, virt), BF16),
            pltpu.VMEM((all_slots, chunk.count, virt), F32),
            pltpu.SemaphoreType.DMA((2 * n_fit,)),
        ],
        compiler_params=params(),
        cost_estimate=cost(
            pairs * (4 * virt**3 + 6 * chunk.count * n_fit * virt * virt),
            pairs * virt * virt * 16,
        ),
        name="middle_step",
    )(slots, fit, *mine, *merged, before, inverse, off)


def gradient_kernel(parts, n, slot_ref, weight_ref, mine_ref, *rest):
    merged = rest[: len(parts)]
    held, sums, sems = rest[-3:]
    outs = rest[-3 - n : -3]
    copies = []
    at = 0
    for (start, offset, rows), ref in zip(parts, merged):
        to = pl.ds(at, rows)
        copies.append(
            pltpu.make_async_copy(
                mine_ref.at[:, pl.ds(start, rows)],
                held.at[pl.ds(0, CAP), to],
                sems.at[len(copies)],
            )
        )
        copies.append(
            pltpu.make_async_copy(
                ref.at[:, pl.ds(offset, rows)],
                held.at[pl.ds(CAP, held.shape[0] - CAP), to],
                sems.at[len(copies)],
            )
        )
        at += rows
    for c in copies:
        c.start()
    for c in copies:
        c.wait()
    add_gradients(slot_ref, weight_ref, lambda s: held[s], sums, outs)


def gradient_chunk(slots, weights, mine, parts, merged, after):
    ends = slots.shape[0]
    virt = mine.shape[2]
    all_slots = CAP + merged[0].shape[0]
    n = all_slots // CAP
    rows = sum(p[2] for p in parts)
    return pl.pallas_call(
        functools.partial(gradient_kernel, parts, n),
        out_shape=[jax.ShapeDtypeStruct((CAP, rows, virt), BF16)] * n,
        in_specs=[SMEM, VMEM, ANY] + [ANY] * (len(parts) + len(after)),
        out_specs=[VMEM] * n,
        scratch_shapes=[
            pltpu.VMEM((all_slots, rows, virt), BF16),
            pltpu.VMEM((all_slots, rows, virt), F32),
            pltpu.SemaphoreType.DMA((2 * len(parts),)),
        ],
        compiler_params=params(),
        cost_estimate=cost(
            2 * ends * rows * virt * virt, 4 * all_slots * rows * virt + ends * virt * virt * 2
        ),
        name="gradient_chunk",
    )(slots, weights, mine, *merged, *after)


def settle_kernel(shape, index_ref, *rest):
    out_ref, sums = rest[-2:]
    sums[...] = jnp.zeros_like(sums)
    at = 0
    for count in shape:
        rows = pl.ds(at, rest[0].shape[1])
        at += rest[0].shape[1]
        for d, ref in enumerate(rest[:count]):
            for k in range(CAP):
                g = index_ref[d, k]
                sums[g, rows] += ref[k].astype(F32)
        rest = rest[count:]
    out_ref[...] = sums[...].astype(BF16)


def settle_chunks(index, returned, local_orbs, after=()):
    rows = sum(r[0].shape[1] for r in returned)
    virt = returned[0][0].shape[2]
    terms = [x for r in returned for x in r]
    return pl.pallas_call(
        functools.partial(settle_kernel, [len(r) for r in returned]),
        out_shape=jax.ShapeDtypeStruct((local_orbs, rows, virt), BF16),
        in_specs=[SMEM] + [VMEM] * len(terms) + [ANY] * len(after),
        out_specs=VMEM,
        scratch_shapes=[pltpu.VMEM((local_orbs, rows, virt), F32)],
        compiler_params=params(),
        cost_estimate=weighed(SETTLE_WEIGHT, 0, (len(returned[0]) * CAP + local_orbs) * 2 * rows * virt),
        name="settle_chunks",
    )(index, *terms, *after)


def add_kernel(groups, *refs):
    count = len(groups)
    grads_ref, wide, sems = refs[-3:]
    copies = []
    at = 0
    for i, group in enumerate(groups):
        mine, other = refs[i], refs[count + i]
        offset = 0
        for c in group:
            rows, source = pl.ds(at, c.count), pl.ds(offset, c.count)
            at, offset = at + c.count, offset + c.count
            for g in range(mine.shape[0]):
                wide[g, rows] = mine[g, source].astype(F32) + other[g, source].astype(F32)
                copies.append(
                    pltpu.make_async_copy(
                        wide.at[g, rows],
                        grads_ref.at[g, pl.ds(c.start, c.count)],
                        sems.at[len(copies)],
                    )
                )
                copies[-1].start()
    for c in copies:
        c.wait()


def add_chunks(waiting, fit_rows, grads=None):
    groups, mine, other = zip(*waiting)
    local_orbs, _, virt = mine[0].shape
    rows = sum(m.shape[1] for m in mine)
    count = len(mine)
    more = [] if grads is None else [grads]
    return pl.pallas_call(
        functools.partial(add_kernel, groups),
        out_shape=jax.ShapeDtypeStruct((local_orbs, fit_rows, virt), F32),
        in_specs=[VMEM] * (2 * count) + [ANY] * len(more),
        out_specs=ANY,
        scratch_shapes=[
            pltpu.VMEM((local_orbs, rows, virt), F32),
            pltpu.SemaphoreType.DMA((local_orbs * sum(len(g) for g in groups),)),
        ],
        input_output_aliases={} if grads is None else {2 * count: 0},
        compiler_params=params(),
        cost_estimate=cost(0, 8 * local_orbs * rows * virt),
        name="add_chunks",
    )(*mine, *other, *more)


def cut_rows(total, weights):
    unit = 16
    units = total // unit
    whole = sum(weights)
    sizes = [max(1, units * w // whole) for w in weights]
    sizes[0] += units - sum(sizes)
    chunks, at = [], 0
    for size in sizes:
        chunks.append(Rows(at, size * unit))
        at += size * unit
    return chunks


def around_fit(x, n_fit):
    return [x] + [lax.ppermute(x, "fit", shifted(n_fit, d)) for d in range(1, n_fit)]


def per_device(blocks, occ_energy, pair_list, pno_sizes, fock_virt):
    n = lax.axis_size("orb")
    n_fit = lax.axis_size("fit")
    n_rep = lax.axis_size("rep")
    local_orbs, fit_rows, virt = blocks.shape
    total_orbs = local_orbs * n
    me = lax.axis_index("orb")

    endpoints = pair_list.reshape(-1)
    relative = (endpoints - me * local_orbs) % total_orbs
    named = jnp.any(
        relative[:, None] == jnp.arange(total_orbs, dtype=jnp.int32)[None, :], axis=0
    ).reshape(n, local_orbs)
    table = named.astype(jnp.int32)
    position = jnp.cumsum(table, axis=1) - 1
    columns = jnp.arange(CAP, dtype=jnp.int32)
    locals_ = jnp.arange(local_orbs, dtype=jnp.int32)
    matches = table[:, :, None] * (position[:, :, None] == columns[None, None, :])
    wanted = jnp.sum(matches * locals_[None, :, None], axis=1)
    end_hot = relative[:, None] == jnp.arange(total_orbs, dtype=jnp.int32)[None, :]
    slots = (relative // local_orbs) * CAP + jnp.sum(
        jnp.where(end_hot, position.reshape(1, -1), 0), axis=1
    )
    slots = slots.astype(jnp.int32)

    energies_here = occ_energy.astype(F32)
    got = {}
    for d in range(1, n):
        note = jnp.concatenate([wanted[d].astype(F32), energies_here])
        got[d] = lax.ppermute(note, "orb", shifted(n, d))
    asked = jnp.stack(
        [wanted[0]] + [got[d][:CAP].astype(jnp.int32) for d in range(1, n)]
    )
    energies = jnp.concatenate([energies_here] + [got[n - d][CAP:] for d in range(1, n)])

    chunks = cut_rows(fit_rows, FORWARD_ROWS)
    fit = lax.axis_index("fit").astype(jnp.int32).reshape(1)
    mine = around_fit(pick_blocks(wanted[:1], blocks, 0, fit_rows)[0], n_fit)
    inverse, off = prepare_pairs(energies, relative, pno_sizes, fock_virt)
    merged, arrived = [], []
    ints = None

    def pass_on(place, after):
        merged.append(around_fit(merge_chunk(arrived[place], after), n_fit))

    def integrals(place, before, after):
        here = slice(place, place + 1)
        return exchange_chunks(slots, fit, chunks[here], mine, merged[here], before, after)

    for place, c in enumerate(chunks):
        after = [mine[0]] if place < 2 else [merged[place - 2][0]]
        picked = pick_blocks(asked[1:], blocks, c.start, c.count, after)
        arrived.append(
            [lax.ppermute(picked[d - 1], "orb", shifted(n, n - d)) for d in range(1, n)]
        )
        if place == 1:
            pass_on(0, [picked[0], inverse])
        elif place == 2:
            pass_on(1, [picked[0]])
        elif place > 2:
            ints = integrals(place - 3, ints, [])
            pass_on(place - 1, [picked[0], ints])
    ints = integrals(len(chunks) - 3, ints, [merged[-1][0]])
    pass_on(len(chunks) - 1, [ints])
    ints = integrals(len(chunks) - 2, ints, [merged[-1][0]])
    amplitudes, weights, *sums = middle_step(
        slots, fit, chunks[-1], mine, merged[-1], ints, inverse, off
    )

    back = [(chunks[-1], sums)]
    for c in reversed(cut_rows(chunks[-1].start, BACK_ROWS)):
        parts, sources = [], []
        for place, chunk in enumerate(chunks[:-1]):
            low = max(c.start, chunk.start)
            high = min(c.start + c.count, chunk.start + chunk.count)
            if low < high:
                parts.append((low, low - chunk.start, high - low))
                sources.append(merged[place][0])
        after = []
        back.append((c, gradient_chunk(slots, weights, mine[0], parts, sources, after)))

    swap = shifted(n_rep, 1)
    waiting = []
    returned = [
        [sums[0]] + [lax.ppermute(sums[d], "orb", shifted(n, d)) for d in range(1, n)]
        for _, sums in back
    ]
    low = 0
    for high in BACK_GROUPS:
        here = settle_chunks(asked, returned[low:high], local_orbs, [w[1] for w in waiting[-1:]])
        group = [c for c, _ in back[low:high]]
        waiting.append((group, here, lax.ppermute(here, "rep", swap)))
        low = high
    grads = add_chunks(waiting[:-1], fit_rows)
    grads = add_chunks(waiting[-1:], fit_rows, grads)
    return amplitudes, grads


def solution(mesh):
    placed = (
        P(("groups", "orb"), "fit", None),
        P(("groups", "orb")),
        P(("groups", "orb", "rep"), None),
        P(("groups", "orb", "rep")),
        P(("groups", "orb", "rep"), None, None),
    )
    return jax.shard_map(
        per_device,
        mesh=mesh,
        in_specs=placed,
        out_specs=(P(("groups", "orb", "rep"), None, None), P(("groups", "orb"), "fit", None)),
        check_vma=False,
    )
```

```python
import functools
from typing import NamedTuple

import jax
import jax.numpy as jnp
from jax import lax
from jax.experimental import pallas as pl
from jax.experimental.pallas import tpu as pltpu
from jax.sharding import PartitionSpec as P

CAP = 2
FORWARD_ROWS = (16, 13, 10, 9, 8, 8)
MIDDLE_CHUNKS = 2
INTEGRAL_LAG = 3
BACK_ROWS = (14, 14, 15, 15)
BACK_GROUPS = (2, 3, 4, 5)
CHAIN_GRADIENTS = False
SETTLE_FROM = 99
SETTLE_WEIGHT = 50
MERGE_WEIGHT = 50
EXCHANGE_WEIGHT = 50
PICK_WEIGHT = 1
PREPARE_WEIGHT = 1
SWAP_FIRST = 9
VMEM_LIMIT = 40 * 1024 * 1024

F32 = jnp.float32
BF16 = jnp.bfloat16

ANY = pl.BlockSpec(memory_space=pl.ANY)
SMEM = pl.BlockSpec(memory_space=pltpu.SMEM)
VMEM = pl.BlockSpec(memory_space=pltpu.VMEM)


def params():
    return pltpu.CompilerParams(vmem_limit_bytes=VMEM_LIMIT)


def cost(flops, nbytes):
    return pl.CostEstimate(flops=int(flops), bytes_accessed=int(nbytes), transcendentals=0)


def weighed(times, flops, nbytes):
    return cost(times * flops, times * nbytes)


def shifted(n, d):
    return [(s, (s + d) % n) for s in range(n)]


def pick_kernel(start, rows, waits, index_ref, blocks_ref, *rest):
    outs, sems = rest[waits:-1], rest[-1]
    copies = []
    for d, out in enumerate(outs):
        for k in range(CAP):
            copies.append(
                pltpu.make_async_copy(
                    blocks_ref.at[index_ref[d, k], pl.ds(start, rows)],
                    out.at[k],
                    sems.at[d * CAP + k],
                )
            )
    for c in copies:
        c.start()
    for c in copies:
        c.wait()


def pick_blocks(index, blocks, start, rows, after=()):
    count = index.shape[0]
    virt = blocks.shape[2]
    shape = jax.ShapeDtypeStruct((CAP, rows, virt), BF16)
    return pl.pallas_call(
        functools.partial(pick_kernel, start, rows, len(after)),
        out_shape=[shape] * count,
        in_specs=[SMEM, ANY] + [ANY] * len(after),
        out_specs=[ANY] * count,
        scratch_shapes=[pltpu.SemaphoreType.DMA((count * CAP,))],
        compiler_params=params(),
        cost_estimate=weighed(PICK_WEIGHT, 0, 2 * count * CAP * rows * virt * 2),
        name="pick_blocks",
    )(index, blocks, *after)


def merge_kernel(count, *refs):
    sources, out, sems = refs[:count], refs[-2], refs[-1]
    copies = [
        pltpu.make_async_copy(ref, out.at[pl.ds(d * CAP, CAP)], sems.at[d])
        for d, ref in enumerate(sources)
    ]
    for c in copies:
        c.start()
    for c in copies:
        c.wait()


def merge_chunk(arrived, after=()):
    count = len(arrived)
    _, rows, virt = arrived[0].shape
    return pl.pallas_call(
        functools.partial(merge_kernel, count),
        out_shape=jax.ShapeDtypeStruct((count * CAP, rows, virt), BF16),
        in_specs=[ANY] * (count + len(after)),
        out_specs=ANY,
        scratch_shapes=[pltpu.SemaphoreType.DMA((count,))],
        compiler_params=params(),
        cost_estimate=weighed(MERGE_WEIGHT, 0, 4 * count * CAP * rows * virt),
        name="merge_chunk",
    )(*arrived, *after)


class Rows(NamedTuple):
    start: int
    count: int


def load_all(fit_ref, chunks, mine, merged, held, sems):
    n_fit = len(mine)
    total = sum(c.count for c in chunks)
    copies = []
    for f in range(n_fit):
        place = lax.rem(fit_ref[0] + (n_fit - f), n_fit)
        at = 0
        for i, c in enumerate(chunks):
            rows = pl.ds(pl.multiple_of(place * total + at, 16), c.count)
            copies.append(
                pltpu.make_async_copy(
                    mine[f].at[:, pl.ds(c.start, c.count)],
                    held.at[pl.ds(0, CAP), rows],
                    sems.at[len(copies)],
                )
            )
            copies.append(
                pltpu.make_async_copy(
                    merged[i][f],
                    held.at[pl.ds(CAP, held.shape[0] - CAP), rows],
                    sems.at[len(copies)],
                )
            )
            at += c.count
    for c in copies:
        c.start()
    return copies


def cross(left, right):
    return lax.dot_general(left, right, (((0,), (0,)), ((), ())), preferred_element_type=F32)


def split_refs(rest, n_fit, chunks):
    mine, rest = rest[:n_fit], rest[n_fit:]
    merged = []
    for _ in chunks:
        merged.append(rest[:n_fit])
        rest = rest[n_fit:]
    return mine, merged, rest


def exchange_kernel(chunks, n_fit, first, waits, slot_ref, fit_ref, *rest):
    mine, merged, rest = split_refs(rest[waits:], n_fit, chunks)
    if not first:
        before_ref, rest = rest[0], rest[1:]
    out_ref, held, sems = rest
    for c in load_all(fit_ref, chunks, mine, merged, held, sems):
        c.wait()

    def step(p, carry):
        product = cross(held[slot_ref[2 * p]], held[slot_ref[2 * p + 1]])
        if not first:
            product = before_ref[p] + product
        out_ref[p] = product
        return carry

    lax.fori_loop(0, out_ref.shape[0], step, 0)


def exchange_chunks(slots, fit, chunks, mine, merged, before, after=()):
    n_fit = len(mine)
    pairs = slots.shape[0] // 2
    virt = mine[0].shape[2]
    all_slots = CAP + merged[0][0].shape[0]
    rows = sum(c.count for c in chunks) * n_fit
    first = before is None
    return pl.pallas_call(
        functools.partial(exchange_kernel, chunks, n_fit, first, len(after)),
        out_shape=jax.ShapeDtypeStruct((pairs, virt, virt), F32),
        in_specs=[SMEM, SMEM]
        + [ANY] * (len(after) + n_fit * (1 + len(chunks)))
        + ([] if first else [VMEM]),
        out_specs=VMEM,
        scratch_shapes=[
            pltpu.VMEM((all_slots, rows, virt), BF16),
            pltpu.SemaphoreType.DMA((2 * n_fit * len(chunks),)),
        ],
        compiler_params=params(),
        cost_estimate=weighed(EXCHANGE_WEIGHT,
            2 * pairs * rows * virt * virt, all_slots * rows * virt * 2 + pairs * virt * virt * 8
        ),
        name="exchange_chunks",
    )(slots, fit, *after, *mine, *[x for m in merged for x in m], *([] if first else [before]))


def prepare_kernel(energy_ref, ends_ref, size_ref, fock_ref, inverse_ref, off_ref):
    p = pl.program_id(0)
    virt = fock_ref.shape[-1]
    occ = energy_ref[ends_ref[2 * p]] + energy_ref[ends_ref[2 * p + 1]]
    size = size_ref[p]
    fock = fock_ref[0]
    row = lax.broadcasted_iota(jnp.int32, (virt, virt), 0)
    col = lax.broadcasted_iota(jnp.int32, (virt, virt), 1)
    on_diagonal = row == col
    diagonal = jnp.where(on_diagonal, fock, 0.0)
    denominator = (
        jnp.sum(diagonal, axis=1, keepdims=True) + jnp.sum(diagonal, axis=0, keepdims=True) - occ
    )
    inverse_ref[0] = jnp.where((row < size) & (col < size), 1.0 / denominator, 0.0)
    off_ref[0] = jnp.where(on_diagonal, 0.0, fock).astype(BF16)


def prepare_pairs(energies, ends, sizes, fock):
    pairs, virt, _ = fock.shape
    block = pl.BlockSpec((1, virt, virt), lambda p: (p, 0, 0))
    return pl.pallas_call(
        prepare_kernel,
        grid=(pairs,),
        out_shape=[
            jax.ShapeDtypeStruct((pairs, virt, virt), F32),
            jax.ShapeDtypeStruct((pairs, virt, virt), BF16),
        ],
        in_specs=[SMEM, SMEM, SMEM, block],
        out_specs=[block, block],
        compiler_params=params(),
        cost_estimate=weighed(PREPARE_WEIGHT, 10 * pairs * virt * virt, pairs * virt * virt * 10),
        name="prepare_pairs",
    )(energies, ends, sizes, fock)


def add_gradients(slot_ref, weight_ref, block_of, sums, outs):
    sums[...] = jnp.zeros_like(sums)

    def step(p, carry):
        left = slot_ref[2 * p]
        right = slot_ref[2 * p + 1]
        sums[left] += jnp.dot(block_of(right), weight_ref[2 * p], preferred_element_type=F32)
        sums[right] += jnp.dot(block_of(left), weight_ref[2 * p + 1], preferred_element_type=F32)
        return carry

    lax.fori_loop(0, weight_ref.shape[0] // 2, step, 0)
    for d, out in enumerate(outs):
        for k in range(CAP):
            out[k] = sums[d * CAP + k].astype(BF16)


def middle_kernel(chunks, n, n_fit, slot_ref, fit_ref, *rest):
    mine, merged, rest = split_refs(rest, n_fit, chunks)
    before_ref, inverse_ref, off_ref, amp_ref, weight_ref = rest[:5]
    outs = rest[5 : 5 + n]
    held, sums, sems = rest[5 + n :]
    for c in load_all(fit_ref, chunks, mine, merged, held, sems):
        c.wait()

    def step(p, carry):
        total = before_ref[p] + cross(held[slot_ref[2 * p]], held[slot_ref[2 * p + 1]])
        inverse = inverse_ref[p]
        off = off_ref[p]
        current = -total * inverse
        rounded = current.astype(BF16)
        change = jnp.dot(off, rounded, preferred_element_type=F32) + jnp.dot(
            rounded, off, preferred_element_type=F32
        )
        amp = (current - change * inverse).astype(BF16)
        amp_ref[p] = amp
        wide = amp.astype(F32)
        flipped = wide.T
        weight_ref[2 * p] = (2.0 * flipped - wide).astype(BF16)
        weight_ref[2 * p + 1] = (2.0 * wide - flipped).astype(BF16)
        return carry

    lax.fori_loop(0, amp_ref.shape[0], step, 0, unroll=2)
    total = sum(c.count for c in chunks)
    last = chunks[-1].count
    here = pl.ds(pl.multiple_of(fit_ref[0] * total + total - last, 16), last)
    add_gradients(slot_ref, weight_ref, lambda s: held[s, here], sums, outs)


def middle_step(slots, fit, chunks, mine, merged, before, inverse, off):
    n_fit = len(mine)
    pairs, virt, _ = before.shape
    all_slots = CAP + merged[0][0].shape[0]
    n = all_slots // CAP
    rows = sum(c.count for c in chunks)
    return pl.pallas_call(
        functools.partial(middle_kernel, chunks, n, n_fit),
        out_shape=[
            jax.ShapeDtypeStruct((pairs, virt, virt), BF16),
            jax.ShapeDtypeStruct((2 * pairs, virt, virt), BF16),
        ]
        + [jax.ShapeDtypeStruct((CAP, chunks[-1].count, virt), BF16)] * n,
        in_specs=[SMEM, SMEM] + [ANY] * (n_fit * (1 + len(chunks))) + [VMEM] * 3,
        out_specs=[VMEM] * (2 + n),
        scratch_shapes=[
            pltpu.VMEM((all_slots, n_fit * rows, virt), BF16),
            pltpu.VMEM((all_slots, chunks[-1].count, virt), F32),
            pltpu.SemaphoreType.DMA((2 * n_fit * len(chunks),)),
        ],
        compiler_params=params(),
        cost_estimate=cost(
            pairs * (4 * virt**3 + 6 * rows * n_fit * virt * virt), pairs * virt * virt * 16
        ),
        name="middle_step",
    )(slots, fit, *mine, *[x for m in merged for x in m], before, inverse, off)


def gradient_kernel(parts, n, slot_ref, weight_ref, mine_ref, *rest):
    merged = rest[: len(parts)]
    held, sums, sems = rest[-3:]
    outs = rest[-3 - n : -3]
    copies = []
    at = 0
    for (start, offset, rows), ref in zip(parts, merged):
        to = pl.ds(at, rows)
        copies.append(
            pltpu.make_async_copy(
                mine_ref.at[:, pl.ds(start, rows)],
                held.at[pl.ds(0, CAP), to],
                sems.at[len(copies)],
            )
        )
        copies.append(
            pltpu.make_async_copy(
                ref.at[:, pl.ds(offset, rows)],
                held.at[pl.ds(CAP, held.shape[0] - CAP), to],
                sems.at[len(copies)],
            )
        )
        at += rows
    for c in copies:
        c.start()
    for c in copies:
        c.wait()
    add_gradients(slot_ref, weight_ref, lambda s: held[s], sums, outs)


def gradient_chunk(slots, weights, mine, parts, merged, after):
    ends = slots.shape[0]
    virt = mine.shape[2]
    all_slots = CAP + merged[0].shape[0]
    n = all_slots // CAP
    rows = sum(p[2] for p in parts)
    return pl.pallas_call(
        functools.partial(gradient_kernel, parts, n),
        out_shape=[jax.ShapeDtypeStruct((CAP, rows, virt), BF16)] * n,
        in_specs=[SMEM, VMEM, ANY] + [ANY] * (len(parts) + len(after)),
        out_specs=[VMEM] * n,
        scratch_shapes=[
            pltpu.VMEM((all_slots, rows, virt), BF16),
            pltpu.VMEM((all_slots, rows, virt), F32),
            pltpu.SemaphoreType.DMA((2 * len(parts),)),
        ],
        compiler_params=params(),
        cost_estimate=cost(
            2 * ends * rows * virt * virt, 4 * all_slots * rows * virt + ends * virt * virt * 2
        ),
        name="gradient_chunk",
    )(slots, weights, mine, *merged, *after)


def settle_kernel(shape, index_ref, *rest):
    out_ref, sums = rest[-2:]
    sums[...] = jnp.zeros_like(sums)
    at = 0
    for count in shape:
        rows = pl.ds(at, rest[0].shape[1])
        at += rest[0].shape[1]
        for d, ref in enumerate(rest[:count]):
            for k in range(CAP):
                g = index_ref[d, k]
                sums[g, rows] += ref[k].astype(F32)
        rest = rest[count:]
    out_ref[...] = sums[...].astype(BF16)


def settle_chunks(index, returned, local_orbs, after=()):
    rows = sum(r[0].shape[1] for r in returned)
    virt = returned[0][0].shape[2]
    terms = [x for r in returned for x in r]
    return pl.pallas_call(
        functools.partial(settle_kernel, [len(r) for r in returned]),
        out_shape=jax.ShapeDtypeStruct((local_orbs, rows, virt), BF16),
        in_specs=[SMEM] + [VMEM] * len(terms) + [ANY] * len(after),
        out_specs=VMEM,
        scratch_shapes=[pltpu.VMEM((local_orbs, rows, virt), F32)],
        compiler_params=params(),
        cost_estimate=weighed(SETTLE_WEIGHT, 0, (len(returned[0]) * CAP + local_orbs) * 2 * rows * virt),
        name="settle_chunks",
    )(index, *terms, *after)


def add_kernel(groups, *refs):
    count = len(groups)
    grads_ref, wide, sems = refs[-3:]
    copies = []
    at = 0
    for i, group in enumerate(groups):
        mine, other = refs[i], refs[count + i]
        offset = 0
        for c in group:
            rows, source = pl.ds(at, c.count), pl.ds(offset, c.count)
            at, offset = at + c.count, offset + c.count
            for g in range(mine.shape[0]):
                wide[g, rows] = mine[g, source].astype(F32) + other[g, source].astype(F32)
                copies.append(
                    pltpu.make_async_copy(
                        wide.at[g, rows],
                        grads_ref.at[g, pl.ds(c.start, c.count)],
                        sems.at[len(copies)],
                    )
                )
                copies[-1].start()
    for c in copies:
        c.wait()


def add_chunks(waiting, fit_rows, grads=None):
    groups, mine, other = zip(*waiting)
    local_orbs, _, virt = mine[0].shape
    rows = sum(m.shape[1] for m in mine)
    count = len(mine)
    more = [] if grads is None else [grads]
    return pl.pallas_call(
        functools.partial(add_kernel, groups),
        out_shape=jax.ShapeDtypeStruct((local_orbs, fit_rows, virt), F32),
        in_specs=[VMEM] * (2 * count) + [ANY] * len(more),
        out_specs=ANY,
        scratch_shapes=[
            pltpu.VMEM((local_orbs, rows, virt), F32),
            pltpu.SemaphoreType.DMA((local_orbs * sum(len(g) for g in groups),)),
        ],
        input_output_aliases={} if grads is None else {2 * count: 0},
        compiler_params=params(),
        cost_estimate=cost(0, 8 * local_orbs * rows * virt),
        name="add_chunks",
    )(*mine, *other, *more)


def cut_rows(total, weights):
    unit = 16
    units = total // unit
    whole = sum(weights)
    sizes = [max(1, units * w // whole) for w in weights]
    sizes[0] += units - sum(sizes)
    chunks, at = [], 0
    for size in sizes:
        chunks.append(Rows(at, size * unit))
        at += size * unit
    return chunks


def around_fit(x, n_fit):
    return [x] + [lax.ppermute(x, "fit", shifted(n_fit, d)) for d in range(1, n_fit)]


def per_device(blocks, occ_energy, pair_list, pno_sizes, fock_virt):
    n = lax.axis_size("orb")
    n_fit = lax.axis_size("fit")
    n_rep = lax.axis_size("rep")
    local_orbs, fit_rows, virt = blocks.shape
    total_orbs = local_orbs * n
    me = lax.axis_index("orb")

    blocks = pltpu.with_memory_space_constraint(blocks, pltpu.HBM)
    endpoints = pair_list.reshape(-1)
    relative = (endpoints - me * local_orbs) % total_orbs
    named = jnp.any(
        relative[:, None] == jnp.arange(total_orbs, dtype=jnp.int32)[None, :], axis=0
    ).reshape(n, local_orbs)
    table = named.astype(jnp.int32)
    position = jnp.cumsum(table, axis=1) - 1
    columns = jnp.arange(CAP, dtype=jnp.int32)
    locals_ = jnp.arange(local_orbs, dtype=jnp.int32)
    matches = table[:, :, None] * (position[:, :, None] == columns[None, None, :])
    wanted = jnp.sum(matches * locals_[None, :, None], axis=1)
    end_hot = relative[:, None] == jnp.arange(total_orbs, dtype=jnp.int32)[None, :]
    slots = (relative // local_orbs) * CAP + jnp.sum(
        jnp.where(end_hot, position.reshape(1, -1), 0), axis=1
    )
    slots = slots.astype(jnp.int32)

    energies_here = occ_energy.astype(F32)
    got = {}
    for d in range(1, n):
        note = jnp.concatenate([wanted[d].astype(F32), energies_here])
        got[d] = lax.ppermute(note, "orb", shifted(n, d))
    asked = jnp.stack(
        [wanted[0]] + [got[d][:CAP].astype(jnp.int32) for d in range(1, n)]
    )
    energies = jnp.concatenate([energies_here] + [got[n - d][CAP:] for d in range(1, n)])

    chunks = cut_rows(fit_rows, FORWARD_ROWS)
    fit = lax.axis_index("fit").astype(jnp.int32).reshape(1)
    mine = around_fit(pick_blocks(wanted[:1], blocks, 0, fit_rows)[0], n_fit)
    inverse, off = prepare_pairs(energies, relative, pno_sizes, fock_virt)
    merged, arrived = [], []
    ints = None

    def pass_on(place, after):
        merged.append(around_fit(merge_chunk(arrived[place], after), n_fit))

    def integrals(place, before, after):
        here = slice(place, place + 1)
        return exchange_chunks(slots, fit, chunks[here], mine, merged[here], before, after)

    count = len(chunks)
    early = count - MIDDLE_CHUNKS
    for place in range(count + 1):
        if place < count:
            c = chunks[place]
            after = [mine[0]] if place < 2 else [merged[place - 2][0]]
            picked = pick_blocks(asked[1:], blocks, c.start, c.count, after)
            arrived.append(
                [lax.ppermute(picked[d - 1], "orb", shifted(n, n - d)) for d in range(1, n)]
            )
        if place > 0:
            after = [picked[0]] if place < count else []
            after += [inverse] if place == 1 else []
            after += merged[-1][1:] if place > SWAP_FIRST else []
            done = place - 1 - INTEGRAL_LAG
            if 0 <= done < early:
                ints = integrals(done, ints, [])
                after.append(ints)
            pass_on(place - 1, after)
    for place in range(max(count - INTEGRAL_LAG, 0), early):
        ints = integrals(place, ints, [merged[-1][0]])
    amplitudes, weights, *sums = middle_step(
        slots, fit, chunks[early:], mine, merged[early:], ints, inverse, off
    )

    first = chunks[-1]
    back = [(first, sums)]
    for c in reversed(cut_rows(first.start, BACK_ROWS)):
        parts, sources = [], []
        for place, chunk in enumerate(chunks[:-1]):
            low = max(c.start, chunk.start)
            high = min(c.start + c.count, chunk.start + chunk.count)
            if low < high:
                parts.append((low, low - chunk.start, high - low))
                sources.append(merged[place][0])
        after = back[-1][1][:1] if CHAIN_GRADIENTS else []
        back.append((c, gradient_chunk(slots, weights, mine[0], parts, sources, after)))

    swap = shifted(n_rep, 1)
    waiting = []
    returned = [
        [sums[0]] + [lax.ppermute(sums[d], "orb", shifted(n, d)) for d in range(1, n)]
        for _, sums in back
    ]
    low = 0
    for high in BACK_GROUPS:
        after = [w[1] for w in waiting[-1:]]
        if high == len(back):
            after = [w[2] for w in waiting[SETTLE_FROM:]]
        here = settle_chunks(asked, returned[low:high], local_orbs, after)
        group = [c for c, _ in back[low:high]]
        waiting.append((group, here, lax.ppermute(here, "rep", swap)))
        low = high
    grads = add_chunks(waiting[:-1], fit_rows)
    grads = add_chunks(waiting[-1:], fit_rows, grads)
    return amplitudes, grads


def solution(mesh):
    placed = (
        P(("groups", "orb"), "fit", None),
        P(("groups", "orb")),
        P(("groups", "orb", "rep"), None),
        P(("groups", "orb", "rep")),
        P(("groups", "orb", "rep"), None, None),
    )
    return jax.shard_map(
        per_device,
        mesh=mesh,
        in_specs=placed,
        out_specs=(P(("groups", "orb", "rep"), None, None), P(("groups", "orb"), "fit", None)),
        check_vma=False,
    )
```

```python
import functools
from typing import NamedTuple

import jax
import jax.numpy as jnp
from jax import lax
from jax.experimental import pallas as pl
from jax.experimental.pallas import tpu as pltpu
from jax.sharding import PartitionSpec as P

CAP = 2
FORWARD_ROWS = (16, 13, 10, 9, 8, 8)
MIDDLE_CHUNKS = 2
INTEGRAL_LAG = 3
BACK_ROWS = (14, 14, 15, 15)
BACK_GROUPS = (2, 3, 4, 5)
CHAIN_GRADIENTS = False
SETTLE_FROM = 99
UNROLL = 4
PREPARE_AT = 3
FIRST_WAITS = (2,)
SETTLE_WEIGHT = 50
MERGE_WEIGHT = 50
EXCHANGE_WEIGHT = 50
PICK_WEIGHT = 1
PREPARE_WEIGHT = 1
SWAP_FIRST = 9
VMEM_LIMIT = 40 * 1024 * 1024

F32 = jnp.float32
BF16 = jnp.bfloat16

ANY = pl.BlockSpec(memory_space=pl.ANY)
SMEM = pl.BlockSpec(memory_space=pltpu.SMEM)
VMEM = pl.BlockSpec(memory_space=pltpu.VMEM)


def params():
    return pltpu.CompilerParams(vmem_limit_bytes=VMEM_LIMIT)


def cost(flops, nbytes):
    return pl.CostEstimate(flops=int(flops), bytes_accessed=int(nbytes), transcendentals=0)


def weighed(times, flops, nbytes):
    return cost(times * flops, times * nbytes)


def shifted(n, d):
    return [(s, (s + d) % n) for s in range(n)]


def pick_kernel(start, rows, waits, index_ref, blocks_ref, *rest):
    outs, sems = rest[waits:-1], rest[-1]
    copies = []
    for d, out in enumerate(outs):
        for k in range(CAP):
            copies.append(
                pltpu.make_async_copy(
                    blocks_ref.at[index_ref[d, k], pl.ds(start, rows)],
                    out.at[k],
                    sems.at[d * CAP + k],
                )
            )
    for c in copies:
        c.start()
    for c in copies:
        c.wait()


def pick_blocks(index, blocks, start, rows, after=()):
    count = index.shape[0]
    virt = blocks.shape[2]
    shape = jax.ShapeDtypeStruct((CAP, rows, virt), BF16)
    return pl.pallas_call(
        functools.partial(pick_kernel, start, rows, len(after)),
        out_shape=[shape] * count,
        in_specs=[SMEM, ANY] + [ANY] * len(after),
        out_specs=[ANY] * count,
        scratch_shapes=[pltpu.SemaphoreType.DMA((count * CAP,))],
        compiler_params=params(),
        cost_estimate=weighed(PICK_WEIGHT, 0, 2 * count * CAP * rows * virt * 2),
        name="pick_blocks",
    )(index, blocks, *after)


def merge_kernel(count, *refs):
    sources, out, sems = refs[:count], refs[-2], refs[-1]
    copies = [
        pltpu.make_async_copy(ref, out.at[pl.ds(d * CAP, CAP)], sems.at[d])
        for d, ref in enumerate(sources)
    ]
    for c in copies:
        c.start()
    for c in copies:
        c.wait()


def merge_chunk(arrived, after=()):
    count = len(arrived)
    _, rows, virt = arrived[0].shape
    return pl.pallas_call(
        functools.partial(merge_kernel, count),
        out_shape=jax.ShapeDtypeStruct((count * CAP, rows, virt), BF16),
        in_specs=[ANY] * (count + len(after)),
        out_specs=ANY,
        scratch_shapes=[pltpu.SemaphoreType.DMA((count,))],
        compiler_params=params(),
        cost_estimate=weighed(MERGE_WEIGHT, 0, 4 * count * CAP * rows * virt),
        name="merge_chunk",
    )(*arrived, *after)


class Rows(NamedTuple):
    start: int
    count: int


def load_all(fit_ref, chunks, mine, merged, held, sems):
    n_fit = len(mine)
    total = sum(c.count for c in chunks)
    copies = []
    for f in range(n_fit):
        place = lax.rem(fit_ref[0] + (n_fit - f), n_fit)
        at = 0
        for i, c in enumerate(chunks):
            rows = pl.ds(pl.multiple_of(place * total + at, 16), c.count)
            copies.append(
                pltpu.make_async_copy(
                    mine[f].at[:, pl.ds(c.start, c.count)],
                    held.at[pl.ds(0, CAP), rows],
                    sems.at[len(copies)],
                )
            )
            copies.append(
                pltpu.make_async_copy(
                    merged[i][f],
                    held.at[pl.ds(CAP, held.shape[0] - CAP), rows],
                    sems.at[len(copies)],
                )
            )
            at += c.count
    for c in copies:
        c.start()
    return copies


def cross(left, right):
    return lax.dot_general(left, right, (((0,), (0,)), ((), ())), preferred_element_type=F32)


def split_refs(rest, n_fit, chunks):
    mine, rest = rest[:n_fit], rest[n_fit:]
    merged = []
    for _ in chunks:
        merged.append(rest[:n_fit])
        rest = rest[n_fit:]
    return mine, merged, rest


def exchange_kernel(chunks, n_fit, first, waits, slot_ref, fit_ref, *rest):
    mine, merged, rest = split_refs(rest[waits:], n_fit, chunks)
    if not first:
        before_ref, rest = rest[0], rest[1:]
    out_ref, held, sems = rest
    for c in load_all(fit_ref, chunks, mine, merged, held, sems):
        c.wait()

    def step(p, carry):
        product = cross(held[slot_ref[2 * p]], held[slot_ref[2 * p + 1]])
        if not first:
            product = before_ref[p] + product
        out_ref[p] = product
        return carry

    lax.fori_loop(0, out_ref.shape[0], step, 0)


def exchange_chunks(slots, fit, chunks, mine, merged, before, after=()):
    n_fit = len(mine)
    pairs = slots.shape[0] // 2
    virt = mine[0].shape[2]
    all_slots = CAP + merged[0][0].shape[0]
    rows = sum(c.count for c in chunks) * n_fit
    first = before is None
    return pl.pallas_call(
        functools.partial(exchange_kernel, chunks, n_fit, first, len(after)),
        out_shape=jax.ShapeDtypeStruct((pairs, virt, virt), F32),
        in_specs=[SMEM, SMEM]
        + [ANY] * (len(after) + n_fit * (1 + len(chunks)))
        + ([] if first else [VMEM]),
        out_specs=VMEM,
        scratch_shapes=[
            pltpu.VMEM((all_slots, rows, virt), BF16),
            pltpu.SemaphoreType.DMA((2 * n_fit * len(chunks),)),
        ],
        compiler_params=params(),
        cost_estimate=weighed(EXCHANGE_WEIGHT,
            2 * pairs * rows * virt * virt, all_slots * rows * virt * 2 + pairs * virt * virt * 8
        ),
        name="exchange_chunks",
    )(slots, fit, *after, *mine, *[x for m in merged for x in m], *([] if first else [before]))


def prepare_kernel(energy_ref, ends_ref, size_ref, fock_ref, inverse_ref, off_ref):
    p = pl.program_id(0)
    virt = fock_ref.shape[-1]
    occ = energy_ref[ends_ref[2 * p]] + energy_ref[ends_ref[2 * p + 1]]
    size = size_ref[p]
    fock = fock_ref[0]
    row = lax.broadcasted_iota(jnp.int32, (virt, virt), 0)
    col = lax.broadcasted_iota(jnp.int32, (virt, virt), 1)
    on_diagonal = row == col
    diagonal = jnp.where(on_diagonal, fock, 0.0)
    denominator = (
        jnp.sum(diagonal, axis=1, keepdims=True) + jnp.sum(diagonal, axis=0, keepdims=True) - occ
    )
    inverse_ref[0] = jnp.where((row < size) & (col < size), 1.0 / denominator, 0.0)
    off_ref[0] = jnp.where(on_diagonal, 0.0, fock).astype(BF16)


def prepare_pairs(energies, ends, sizes, fock):
    pairs, virt, _ = fock.shape
    block = pl.BlockSpec((1, virt, virt), lambda p: (p, 0, 0))
    return pl.pallas_call(
        prepare_kernel,
        grid=(pairs,),
        out_shape=[
            jax.ShapeDtypeStruct((pairs, virt, virt), F32),
            jax.ShapeDtypeStruct((pairs, virt, virt), BF16),
        ],
        in_specs=[SMEM, SMEM, SMEM, block],
        out_specs=[block, block],
        compiler_params=params(),
        cost_estimate=weighed(PREPARE_WEIGHT, 10 * pairs * virt * virt, pairs * virt * virt * 10),
        name="prepare_pairs",
    )(energies, ends, sizes, fock)


def add_gradients(slot_ref, weight_ref, block_of, sums, outs):
    sums[...] = jnp.zeros_like(sums)

    def step(p, carry):
        left = slot_ref[2 * p]
        right = slot_ref[2 * p + 1]
        sums[left] += jnp.dot(block_of(right), weight_ref[2 * p], preferred_element_type=F32)
        sums[right] += jnp.dot(block_of(left), weight_ref[2 * p + 1], preferred_element_type=F32)
        return carry

    lax.fori_loop(0, weight_ref.shape[0] // 2, step, 0)
    for d, out in enumerate(outs):
        for k in range(CAP):
            out[k] = sums[d * CAP + k].astype(BF16)


def middle_kernel(chunks, n, n_fit, slot_ref, fit_ref, *rest):
    mine, merged, rest = split_refs(rest, n_fit, chunks)
    before_ref, inverse_ref, off_ref, amp_ref, weight_ref = rest[:5]
    outs = rest[5 : 5 + n]
    held, sums, sems = rest[5 + n :]
    for c in load_all(fit_ref, chunks, mine, merged, held, sems):
        c.wait()

    def step(p, carry):
        total = before_ref[p] + cross(held[slot_ref[2 * p]], held[slot_ref[2 * p + 1]])
        inverse = inverse_ref[p]
        off = off_ref[p]
        current = -total * inverse
        rounded = current.astype(BF16)
        change = jnp.dot(off, rounded, preferred_element_type=F32) + jnp.dot(
            rounded, off, preferred_element_type=F32
        )
        amp = (current - change * inverse).astype(BF16)
        amp_ref[p] = amp
        wide = amp.astype(F32)
        flipped = wide.T
        weight_ref[2 * p] = (2.0 * flipped - wide).astype(BF16)
        weight_ref[2 * p + 1] = (2.0 * wide - flipped).astype(BF16)
        return carry

    lax.fori_loop(0, amp_ref.shape[0], step, 0, unroll=UNROLL)
    total = sum(c.count for c in chunks)
    last = chunks[-1].count
    here = pl.ds(pl.multiple_of(fit_ref[0] * total + total - last, 16), last)
    add_gradients(slot_ref, weight_ref, lambda s: held[s, here], sums, outs)


def middle_step(slots, fit, chunks, mine, merged, before, inverse, off):
    n_fit = len(mine)
    pairs, virt, _ = before.shape
    all_slots = CAP + merged[0][0].shape[0]
    n = all_slots // CAP
    rows = sum(c.count for c in chunks)
    return pl.pallas_call(
        functools.partial(middle_kernel, chunks, n, n_fit),
        out_shape=[
            jax.ShapeDtypeStruct((pairs, virt, virt), BF16),
            jax.ShapeDtypeStruct((2 * pairs, virt, virt), BF16),
        ]
        + [jax.ShapeDtypeStruct((CAP, chunks[-1].count, virt), BF16)] * n,
        in_specs=[SMEM, SMEM] + [ANY] * (n_fit * (1 + len(chunks))) + [VMEM] * 3,
        out_specs=[VMEM] * (2 + n),
        scratch_shapes=[
            pltpu.VMEM((all_slots, n_fit * rows, virt), BF16),
            pltpu.VMEM((all_slots, chunks[-1].count, virt), F32),
            pltpu.SemaphoreType.DMA((2 * n_fit * len(chunks),)),
        ],
        compiler_params=params(),
        cost_estimate=cost(
            pairs * (4 * virt**3 + 6 * rows * n_fit * virt * virt), pairs * virt * virt * 16
        ),
        name="middle_step",
    )(slots, fit, *mine, *[x for m in merged for x in m], before, inverse, off)


def gradient_kernel(parts, n, slot_ref, weight_ref, mine_ref, *rest):
    merged = rest[: len(parts)]
    held, sums, sems = rest[-3:]
    outs = rest[-3 - n : -3]
    copies = []
    at = 0
    for (start, offset, rows), ref in zip(parts, merged):
        to = pl.ds(at, rows)
        copies.append(
            pltpu.make_async_copy(
                mine_ref.at[:, pl.ds(start, rows)],
                held.at[pl.ds(0, CAP), to],
                sems.at[len(copies)],
            )
        )
        copies.append(
            pltpu.make_async_copy(
                ref.at[:, pl.ds(offset, rows)],
                held.at[pl.ds(CAP, held.shape[0] - CAP), to],
                sems.at[len(copies)],
            )
        )
        at += rows
    for c in copies:
        c.start()
    for c in copies:
        c.wait()
    add_gradients(slot_ref, weight_ref, lambda s: held[s], sums, outs)


def gradient_chunk(slots, weights, mine, parts, merged, after):
    ends = slots.shape[0]
    virt = mine.shape[2]
    all_slots = CAP + merged[0].shape[0]
    n = all_slots // CAP
    rows = sum(p[2] for p in parts)
    return pl.pallas_call(
        functools.partial(gradient_kernel, parts, n),
        out_shape=[jax.ShapeDtypeStruct((CAP, rows, virt), BF16)] * n,
        in_specs=[SMEM, VMEM, ANY] + [ANY] * (len(parts) + len(after)),
        out_specs=[VMEM] * n,
        scratch_shapes=[
            pltpu.VMEM((all_slots, rows, virt), BF16),
            pltpu.VMEM((all_slots, rows, virt), F32),
            pltpu.SemaphoreType.DMA((2 * len(parts),)),
        ],
        compiler_params=params(),
        cost_estimate=cost(
            2 * ends * rows * virt * virt, 4 * all_slots * rows * virt + ends * virt * virt * 2
        ),
        name="gradient_chunk",
    )(slots, weights, mine, *merged, *after)


def settle_kernel(shape, index_ref, *rest):
    out_ref, sums = rest[-2:]
    sums[...] = jnp.zeros_like(sums)
    at = 0
    for count in shape:
        rows = pl.ds(at, rest[0].shape[1])
        at += rest[0].shape[1]
        for d, ref in enumerate(rest[:count]):
            for k in range(CAP):
                g = index_ref[d, k]
                sums[g, rows] += ref[k].astype(F32)
        rest = rest[count:]
    out_ref[...] = sums[...].astype(BF16)


def settle_chunks(index, returned, local_orbs, after=()):
    rows = sum(r[0].shape[1] for r in returned)
    virt = returned[0][0].shape[2]
    terms = [x for r in returned for x in r]
    return pl.pallas_call(
        functools.partial(settle_kernel, [len(r) for r in returned]),
        out_shape=jax.ShapeDtypeStruct((local_orbs, rows, virt), BF16),
        in_specs=[SMEM] + [VMEM] * len(terms) + [ANY] * len(after),
        out_specs=VMEM,
        scratch_shapes=[pltpu.VMEM((local_orbs, rows, virt), F32)],
        compiler_params=params(),
        cost_estimate=weighed(SETTLE_WEIGHT, 0, (len(returned[0]) * CAP + local_orbs) * 2 * rows * virt),
        name="settle_chunks",
    )(index, *terms, *after)


def add_kernel(groups, *refs):
    count = len(groups)
    grads_ref, wide, sems = refs[-3:]
    copies = []
    at = 0
    for i, group in enumerate(groups):
        mine, other = refs[i], refs[count + i]
        offset = 0
        for c in group:
            rows, source = pl.ds(at, c.count), pl.ds(offset, c.count)
            at, offset = at + c.count, offset + c.count
            for g in range(mine.shape[0]):
                wide[g, rows] = mine[g, source].astype(F32) + other[g, source].astype(F32)
                copies.append(
                    pltpu.make_async_copy(
                        wide.at[g, rows],
                        grads_ref.at[g, pl.ds(c.start, c.count)],
                        sems.at[len(copies)],
                    )
                )
                copies[-1].start()
    for c in copies:
        c.wait()


def add_chunks(waiting, fit_rows, grads=None):
    groups, mine, other = zip(*waiting)
    local_orbs, _, virt = mine[0].shape
    rows = sum(m.shape[1] for m in mine)
    count = len(mine)
    more = [] if grads is None else [grads]
    return pl.pallas_call(
        functools.partial(add_kernel, groups),
        out_shape=jax.ShapeDtypeStruct((local_orbs, fit_rows, virt), F32),
        in_specs=[VMEM] * (2 * count) + [ANY] * len(more),
        out_specs=ANY,
        scratch_shapes=[
            pltpu.VMEM((local_orbs, rows, virt), F32),
            pltpu.SemaphoreType.DMA((local_orbs * sum(len(g) for g in groups),)),
        ],
        input_output_aliases={} if grads is None else {2 * count: 0},
        compiler_params=params(),
        cost_estimate=cost(0, 8 * local_orbs * rows * virt),
        name="add_chunks",
    )(*mine, *other, *more)


def cut_rows(total, weights):
    unit = 16
    units = total // unit
    whole = sum(weights)
    sizes = [max(1, units * w // whole) for w in weights]
    sizes[0] += units - sum(sizes)
    chunks, at = [], 0
    for size in sizes:
        chunks.append(Rows(at, size * unit))
        at += size * unit
    return chunks


def around_fit(x, n_fit):
    return [x] + [lax.ppermute(x, "fit", shifted(n_fit, d)) for d in range(1, n_fit)]


def per_device(blocks, occ_energy, pair_list, pno_sizes, fock_virt):
    n = lax.axis_size("orb")
    n_fit = lax.axis_size("fit")
    n_rep = lax.axis_size("rep")
    local_orbs, fit_rows, virt = blocks.shape
    total_orbs = local_orbs * n
    me = lax.axis_index("orb")

    blocks = pltpu.with_memory_space_constraint(blocks, pltpu.HBM)
    endpoints = pair_list.reshape(-1)
    relative = (endpoints - me * local_orbs) % total_orbs
    named = jnp.any(
        relative[:, None] == jnp.arange(total_orbs, dtype=jnp.int32)[None, :], axis=0
    ).reshape(n, local_orbs)
    table = named.astype(jnp.int32)
    position = jnp.cumsum(table, axis=1) - 1
    columns = jnp.arange(CAP, dtype=jnp.int32)
    locals_ = jnp.arange(local_orbs, dtype=jnp.int32)
    matches = table[:, :, None] * (position[:, :, None] == columns[None, None, :])
    wanted = jnp.sum(matches * locals_[None, :, None], axis=1)
    end_hot = relative[:, None] == jnp.arange(total_orbs, dtype=jnp.int32)[None, :]
    slots = (relative // local_orbs) * CAP + jnp.sum(
        jnp.where(end_hot, position.reshape(1, -1), 0), axis=1
    )
    slots = slots.astype(jnp.int32)

    energies_here = occ_energy.astype(F32)
    got = {}
    for d in range(1, n):
        note = jnp.concatenate([wanted[d].astype(F32), energies_here])
        got[d] = lax.ppermute(note, "orb", shifted(n, d))
    asked = jnp.stack(
        [wanted[0]] + [got[d][:CAP].astype(jnp.int32) for d in range(1, n)]
    )
    energies = jnp.concatenate([energies_here] + [got[n - d][CAP:] for d in range(1, n)])

    chunks = cut_rows(fit_rows, FORWARD_ROWS)
    fit = lax.axis_index("fit").astype(jnp.int32).reshape(1)
    mine = around_fit(pick_blocks(wanted[:1], blocks, 0, fit_rows)[0], n_fit)
    inverse, off = prepare_pairs(energies, relative, pno_sizes, fock_virt)
    merged, arrived = [], []
    ints = None

    def pass_on(place, after):
        merged.append(around_fit(merge_chunk(arrived[place], after), n_fit))

    def integrals(place, before, after):
        here = slice(place, place + 1)
        return exchange_chunks(slots, fit, chunks[here], mine, merged[here], before, after)

    count = len(chunks)
    early = count - MIDDLE_CHUNKS
    for place in range(count + 1):
        if place < count:
            c = chunks[place]
            after = [mine[0]] if place < 2 else [merged[place - 2][0]]
            picked = pick_blocks(asked[1:], blocks, c.start, c.count, after)
            arrived.append(
                [lax.ppermute(picked[d - 1], "orb", shifted(n, n - d)) for d in range(1, n)]
            )
        if place > 0:
            after = [picked[0]] if place < count else []
            after += [inverse] if place == PREPARE_AT else []
            after += [arrived[1][j] for j in FIRST_WAITS] if place == 1 else []
            after += merged[-1][1:] if place > SWAP_FIRST else []
            done = place - 1 - INTEGRAL_LAG
            if 0 <= done < early:
                ints = integrals(done, ints, [])
                after.append(ints)
            pass_on(place - 1, after)
    for place in range(max(count - INTEGRAL_LAG, 0), early):
        ints = integrals(place, ints, [merged[-1][0]])
    amplitudes, weights, *sums = middle_step(
        slots, fit, chunks[early:], mine, merged[early:], ints, inverse, off
    )

    first = chunks[-1]
    back = [(first, sums)]
    for c in reversed(cut_rows(first.start, BACK_ROWS)):
        parts, sources = [], []
        for place, chunk in enumerate(chunks[:-1]):
            low = max(c.start, chunk.start)
            high = min(c.start + c.count, chunk.start + chunk.count)
            if low < high:
                parts.append((low, low - chunk.start, high - low))
                sources.append(merged[place][0])
        after = back[-1][1][:1] if CHAIN_GRADIENTS else []
        back.append((c, gradient_chunk(slots, weights, mine[0], parts, sources, after)))

    swap = shifted(n_rep, 1)
    waiting = []
    returned = [
        [sums[0]] + [lax.ppermute(sums[d], "orb", shifted(n, d)) for d in range(1, n)]
        for _, sums in back
    ]
    low = 0
    for high in BACK_GROUPS:
        after = [w[1] for w in waiting[-1:]]
        if high == len(back):
            after = [w[2] for w in waiting[SETTLE_FROM:]]
        here = settle_chunks(asked, returned[low:high], local_orbs, after)
        group = [c for c, _ in back[low:high]]
        waiting.append((group, here, lax.ppermute(here, "rep", swap)))
        low = high
    grads = add_chunks(waiting[:-1], fit_rows)
    grads = add_chunks(waiting[-1:], fit_rows, grads)
    return amplitudes, grads


def solution(mesh):
    placed = (
        P(("groups", "orb"), "fit", None),
        P(("groups", "orb")),
        P(("groups", "orb", "rep"), None),
        P(("groups", "orb", "rep")),
        P(("groups", "orb", "rep"), None, None),
    )
    return jax.shard_map(
        per_device,
        mesh=mesh,
        in_specs=placed,
        out_specs=(P(("groups", "orb", "rep"), None, None), P(("groups", "orb"), "fit", None)),
        check_vma=False,
    )
```

```python
import functools
from typing import NamedTuple

import jax
import jax.numpy as jnp
from jax import lax
from jax.experimental import pallas as pl
from jax.experimental.pallas import tpu as pltpu
from jax.sharding import PartitionSpec as P

CAP = 2
FORWARD_ROWS = (16, 13, 10, 9, 8, 8)
MIDDLE_CHUNKS = 2
INTEGRAL_LAG = 3
BACK_ROWS = (14, 14, 15, 15)
BACK_GROUPS = (2, 3, 4, 5)
CHAIN_GRADIENTS = False
SETTLE_FROM = 99
UNROLL = 4
PREPARE_AT = 3
FIRST_WAITS = (2,)
SETTLE_WEIGHT = 50
MERGE_WEIGHT = 50
EXCHANGE_WEIGHT = 50
PICK_WEIGHT = 1
PREPARE_WEIGHT = 1
SWAP_FIRST = 9
VMEM_LIMIT = 40 * 1024 * 1024

F32 = jnp.float32
BF16 = jnp.bfloat16

ANY = pl.BlockSpec(memory_space=pl.ANY)
SMEM = pl.BlockSpec(memory_space=pltpu.SMEM)
VMEM = pl.BlockSpec(memory_space=pltpu.VMEM)


def params():
    return pltpu.CompilerParams(vmem_limit_bytes=VMEM_LIMIT)


def cost(flops, nbytes):
    return pl.CostEstimate(flops=int(flops), bytes_accessed=int(nbytes), transcendentals=0)


def weighed(times, flops, nbytes):
    return cost(times * flops, times * nbytes)


def shifted(n, d):
    return [(s, (s + d) % n) for s in range(n)]


def pick_kernel(start, rows, waits, index_ref, blocks_ref, *rest):
    outs, sems = rest[waits:-1], rest[-1]
    copies = []
    for d, out in enumerate(outs):
        for k in range(CAP):
            copies.append(
                pltpu.make_async_copy(
                    blocks_ref.at[index_ref[d, k], pl.ds(start, rows)],
                    out.at[k],
                    sems.at[d * CAP + k],
                )
            )
    for c in copies:
        c.start()
    for c in copies:
        c.wait()


def pick_blocks(index, blocks, start, rows, after=()):
    count = index.shape[0]
    virt = blocks.shape[2]
    shape = jax.ShapeDtypeStruct((CAP, rows, virt), BF16)
    return pl.pallas_call(
        functools.partial(pick_kernel, start, rows, len(after)),
        out_shape=[shape] * count,
        in_specs=[SMEM, ANY] + [ANY] * len(after),
        out_specs=[ANY] * count,
        scratch_shapes=[pltpu.SemaphoreType.DMA((count * CAP,))],
        compiler_params=params(),
        cost_estimate=weighed(PICK_WEIGHT, 0, 2 * count * CAP * rows * virt * 2),
        name="pick_blocks",
    )(index, blocks, *after)


def merge_kernel(count, *refs):
    sources, out, sems = refs[:count], refs[-2], refs[-1]
    copies = [
        pltpu.make_async_copy(ref, out.at[pl.ds(d * CAP, CAP)], sems.at[d])
        for d, ref in enumerate(sources)
    ]
    for c in copies:
        c.start()
    for c in copies:
        c.wait()


def merge_chunk(arrived, after=()):
    count = len(arrived)
    _, rows, virt = arrived[0].shape
    return pl.pallas_call(
        functools.partial(merge_kernel, count),
        out_shape=jax.ShapeDtypeStruct((count * CAP, rows, virt), BF16),
        in_specs=[ANY] * (count + len(after)),
        out_specs=ANY,
        scratch_shapes=[pltpu.SemaphoreType.DMA((count,))],
        compiler_params=params(),
        cost_estimate=weighed(MERGE_WEIGHT, 0, 4 * count * CAP * rows * virt),
        name="merge_chunk",
    )(*arrived, *after)


class Rows(NamedTuple):
    start: int
    count: int


def load_all(fit_ref, chunks, mine, merged, held, sems):
    n_fit = len(mine)
    total = sum(c.count for c in chunks)
    copies = []
    for f in range(n_fit):
        place = lax.rem(fit_ref[0] + (n_fit - f), n_fit)
        at = 0
        for i, c in enumerate(chunks):
            rows = pl.ds(pl.multiple_of(place * total + at, 16), c.count)
            copies.append(
                pltpu.make_async_copy(
                    mine[f].at[:, pl.ds(c.start, c.count)],
                    held.at[pl.ds(0, CAP), rows],
                    sems.at[len(copies)],
                )
            )
            copies.append(
                pltpu.make_async_copy(
                    merged[i][f],
                    held.at[pl.ds(CAP, held.shape[0] - CAP), rows],
                    sems.at[len(copies)],
                )
            )
            at += c.count
    for c in copies:
        c.start()
    return copies


def cross(left, right):
    return lax.dot_general(left, right, (((0,), (0,)), ((), ())), preferred_element_type=F32)


def split_refs(rest, n_fit, chunks):
    mine, rest = rest[:n_fit], rest[n_fit:]
    merged = []
    for _ in chunks:
        merged.append(rest[:n_fit])
        rest = rest[n_fit:]
    return mine, merged, rest


def exchange_kernel(chunks, n_fit, first, waits, slot_ref, fit_ref, *rest):
    mine, merged, rest = split_refs(rest[waits:], n_fit, chunks)
    if not first:
        before_ref, rest = rest[0], rest[1:]
    out_ref, held, sems = rest
    for c in load_all(fit_ref, chunks, mine, merged, held, sems):
        c.wait()

    def step(p, carry):
        product = cross(held[slot_ref[2 * p]], held[slot_ref[2 * p + 1]])
        if not first:
            product = before_ref[p] + product
        out_ref[p] = product
        return carry

    lax.fori_loop(0, out_ref.shape[0], step, 0)


def exchange_chunks(slots, fit, chunks, mine, merged, before, after=()):
    n_fit = len(mine)
    pairs = slots.shape[0] // 2
    virt = mine[0].shape[2]
    all_slots = CAP + merged[0][0].shape[0]
    rows = sum(c.count for c in chunks) * n_fit
    first = before is None
    return pl.pallas_call(
        functools.partial(exchange_kernel, chunks, n_fit, first, len(after)),
        out_shape=jax.ShapeDtypeStruct((pairs, virt, virt), F32),
        in_specs=[SMEM, SMEM]
        + [ANY] * (len(after) + n_fit * (1 + len(chunks)))
        + ([] if first else [VMEM]),
        out_specs=VMEM,
        scratch_shapes=[
            pltpu.VMEM((all_slots, rows, virt), BF16),
            pltpu.SemaphoreType.DMA((2 * n_fit * len(chunks),)),
        ],
        compiler_params=params(),
        cost_estimate=weighed(EXCHANGE_WEIGHT,
            2 * pairs * rows * virt * virt, all_slots * rows * virt * 2 + pairs * virt * virt * 8
        ),
        name="exchange_chunks",
    )(slots, fit, *after, *mine, *[x for m in merged for x in m], *([] if first else [before]))


def prepare_kernel(energy_ref, ends_ref, size_ref, fock_ref, inverse_ref, off_ref):
    p = pl.program_id(0)
    virt = fock_ref.shape[-1]
    occ = energy_ref[ends_ref[2 * p]] + energy_ref[ends_ref[2 * p + 1]]
    size = size_ref[p]
    fock = fock_ref[0]
    row = lax.broadcasted_iota(jnp.int32, (virt, virt), 0)
    col = lax.broadcasted_iota(jnp.int32, (virt, virt), 1)
    on_diagonal = row == col
    diagonal = jnp.where(on_diagonal, fock, 0.0)
    denominator = (
        jnp.sum(diagonal, axis=1, keepdims=True) + jnp.sum(diagonal, axis=0, keepdims=True) - occ
    )
    inverse_ref[0] = jnp.where((row < size) & (col < size), 1.0 / denominator, 0.0)
    off_ref[0] = jnp.where(on_diagonal, 0.0, fock).astype(BF16)


def prepare_pairs(energies, ends, sizes, fock):
    pairs, virt, _ = fock.shape
    block = pl.BlockSpec((1, virt, virt), lambda p: (p, 0, 0))
    return pl.pallas_call(
        prepare_kernel,
        grid=(pairs,),
        out_shape=[
            jax.ShapeDtypeStruct((pairs, virt, virt), F32),
            jax.ShapeDtypeStruct((pairs, virt, virt), BF16),
        ],
        in_specs=[SMEM, SMEM, SMEM, block],
        out_specs=[block, block],
        compiler_params=params(),
        cost_estimate=weighed(PREPARE_WEIGHT, 10 * pairs * virt * virt, pairs * virt * virt * 10),
        name="prepare_pairs",
    )(energies, ends, sizes, fock)


def add_gradients(slot_ref, weight_ref, block_of, sums, outs):
    sums[...] = jnp.zeros_like(sums)

    def step(p, carry):
        left = slot_ref[2 * p]
        right = slot_ref[2 * p + 1]
        sums[left] += jnp.dot(block_of(right), weight_ref[2 * p], preferred_element_type=F32)
        sums[right] += jnp.dot(block_of(left), weight_ref[2 * p + 1], preferred_element_type=F32)
        return carry

    lax.fori_loop(0, weight_ref.shape[0] // 2, step, 0)
    for d, out in enumerate(outs):
        for k in range(CAP):
            out[k] = sums[d * CAP + k].astype(BF16)


def middle_kernel(chunks, n, n_fit, slot_ref, fit_ref, *rest):
    mine, merged, rest = split_refs(rest, n_fit, chunks)
    before_ref, inverse_ref, off_ref, amp_ref, weight_ref = rest[:5]
    outs = rest[5 : 5 + n]
    held, sums, sems = rest[5 + n :]
    for c in load_all(fit_ref, chunks, mine, merged, held, sems):
        c.wait()

    def step(p, carry):
        total = before_ref[p] + cross(held[slot_ref[2 * p]], held[slot_ref[2 * p + 1]])
        inverse = inverse_ref[p]
        off = off_ref[p]
        current = -total * inverse
        rounded = current.astype(BF16)
        change = jnp.dot(off, rounded, preferred_element_type=F32) + jnp.dot(
            rounded, off, preferred_element_type=F32
        )
        amp = (current - change * inverse).astype(BF16)
        amp_ref[p] = amp
        wide = amp.astype(F32)
        flipped = wide.T
        weight_ref[2 * p] = (2.0 * flipped - wide).astype(BF16)
        weight_ref[2 * p + 1] = (2.0 * wide - flipped).astype(BF16)
        return carry

    lax.fori_loop(0, amp_ref.shape[0], step, 0, unroll=UNROLL)
    total = sum(c.count for c in chunks)
    last = chunks[-1].count
    here = pl.ds(pl.multiple_of(fit_ref[0] * total + total - last, 16), last)
    add_gradients(slot_ref, weight_ref, lambda s: held[s, here], sums, outs)


def middle_step(slots, fit, chunks, mine, merged, before, inverse, off):
    n_fit = len(mine)
    pairs, virt, _ = before.shape
    all_slots = CAP + merged[0][0].shape[0]
    n = all_slots // CAP
    rows = sum(c.count for c in chunks)
    return pl.pallas_call(
        functools.partial(middle_kernel, chunks, n, n_fit),
        out_shape=[
            jax.ShapeDtypeStruct((pairs, virt, virt), BF16),
            jax.ShapeDtypeStruct((2 * pairs, virt, virt), BF16),
        ]
        + [jax.ShapeDtypeStruct((CAP, chunks[-1].count, virt), BF16)] * n,
        in_specs=[SMEM, SMEM] + [ANY] * (n_fit * (1 + len(chunks))) + [VMEM] * 3,
        out_specs=[VMEM] * (2 + n),
        scratch_shapes=[
            pltpu.VMEM((all_slots, n_fit * rows, virt), BF16),
            pltpu.VMEM((all_slots, chunks[-1].count, virt), F32),
            pltpu.SemaphoreType.DMA((2 * n_fit * len(chunks),)),
        ],
        compiler_params=params(),
        cost_estimate=cost(
            pairs * (4 * virt**3 + 6 * rows * n_fit * virt * virt), pairs * virt * virt * 16
        ),
        name="middle_step",
    )(slots, fit, *mine, *[x for m in merged for x in m], before, inverse, off)


def gradient_kernel(parts, n, slot_ref, weight_ref, mine_ref, *rest):
    merged = rest[: len(parts)]
    held, sums, sems = rest[-3:]
    outs = rest[-3 - n : -3]
    copies = []
    at = 0
    for (start, offset, rows), ref in zip(parts, merged):
        to = pl.ds(at, rows)
        copies.append(
            pltpu.make_async_copy(
                mine_ref.at[:, pl.ds(start, rows)],
                held.at[pl.ds(0, CAP), to],
                sems.at[len(copies)],
            )
        )
        copies.append(
            pltpu.make_async_copy(
                ref.at[:, pl.ds(offset, rows)],
                held.at[pl.ds(CAP, held.shape[0] - CAP), to],
                sems.at[len(copies)],
            )
        )
        at += rows
    for c in copies:
        c.start()
    for c in copies:
        c.wait()
    add_gradients(slot_ref, weight_ref, lambda s: held[s], sums, outs)


def gradient_chunk(slots, weights, mine, parts, merged, after):
    ends = slots.shape[0]
    virt = mine.shape[2]
    all_slots = CAP + merged[0].shape[0]
    n = all_slots // CAP
    rows = sum(p[2] for p in parts)
    return pl.pallas_call(
        functools.partial(gradient_kernel, parts, n),
        out_shape=[jax.ShapeDtypeStruct((CAP, rows, virt), BF16)] * n,
        in_specs=[SMEM, VMEM, ANY] + [ANY] * (len(parts) + len(after)),
        out_specs=[VMEM] * n,
        scratch_shapes=[
            pltpu.VMEM((all_slots, rows, virt), BF16),
            pltpu.VMEM((all_slots, rows, virt), F32),
            pltpu.SemaphoreType.DMA((2 * len(parts),)),
        ],
        compiler_params=params(),
        cost_estimate=cost(
            2 * ends * rows * virt * virt, 4 * all_slots * rows * virt + ends * virt * virt * 2
        ),
        name="gradient_chunk",
    )(slots, weights, mine, *merged, *after)


def settle_kernel(shape, index_ref, *rest):
    out_ref, sums = rest[-2:]
    sums[...] = jnp.zeros_like(sums)
    at = 0
    for count in shape:
        rows = pl.ds(at, rest[0].shape[1])
        at += rest[0].shape[1]
        for d, ref in enumerate(rest[:count]):
            for k in range(CAP):
                g = index_ref[d, k]
                sums[g, rows] += ref[k].astype(F32)
        rest = rest[count:]
    out_ref[...] = sums[...].astype(BF16)


def settle_chunks(index, returned, local_orbs, after=()):
    rows = sum(r[0].shape[1] for r in returned)
    virt = returned[0][0].shape[2]
    terms = [x for r in returned for x in r]
    return pl.pallas_call(
        functools.partial(settle_kernel, [len(r) for r in returned]),
        out_shape=jax.ShapeDtypeStruct((local_orbs, rows, virt), BF16),
        in_specs=[SMEM] + [VMEM] * len(terms) + [ANY] * len(after),
        out_specs=VMEM,
        scratch_shapes=[pltpu.VMEM((local_orbs, rows, virt), F32)],
        compiler_params=params(),
        cost_estimate=weighed(SETTLE_WEIGHT, 0, (len(returned[0]) * CAP + local_orbs) * 2 * rows * virt),
        name="settle_chunks",
    )(index, *terms, *after)


def add_kernel(groups, *refs):
    count = len(groups)
    grads_ref, wide, sems = refs[-3:]
    copies = []
    at = 0
    for i, group in enumerate(groups):
        mine, other = refs[i], refs[count + i]
        offset = 0
        for c in group:
            rows, source = pl.ds(at, c.count), pl.ds(offset, c.count)
            at, offset = at + c.count, offset + c.count
            for g in range(mine.shape[0]):
                wide[g, rows] = mine[g, source].astype(F32) + other[g, source].astype(F32)
                copies.append(
                    pltpu.make_async_copy(
                        wide.at[g, rows],
                        grads_ref.at[g, pl.ds(c.start, c.count)],
                        sems.at[len(copies)],
                    )
                )
                copies[-1].start()
    for c in copies:
        c.wait()


def add_chunks(waiting, fit_rows, grads=None):
    groups, mine, other = zip(*waiting)
    local_orbs, _, virt = mine[0].shape
    rows = sum(m.shape[1] for m in mine)
    count = len(mine)
    more = [] if grads is None else [grads]
    return pl.pallas_call(
        functools.partial(add_kernel, groups),
        out_shape=jax.ShapeDtypeStruct((local_orbs, fit_rows, virt), F32),
        in_specs=[VMEM] * (2 * count) + [ANY] * len(more),
        out_specs=ANY,
        scratch_shapes=[
            pltpu.VMEM((local_orbs, rows, virt), F32),
            pltpu.SemaphoreType.DMA((local_orbs * sum(len(g) for g in groups),)),
        ],
        input_output_aliases={} if grads is None else {2 * count: 0},
        compiler_params=params(),
        cost_estimate=cost(0, 8 * local_orbs * rows * virt),
        name="add_chunks",
    )(*mine, *other, *more)


def cut_rows(total, weights):
    unit = 16
    units = total // unit
    whole = sum(weights)
    sizes = [max(1, units * w // whole) for w in weights]
    sizes[0] += units - sum(sizes)
    chunks, at = [], 0
    for size in sizes:
        chunks.append(Rows(at, size * unit))
        at += size * unit
    return chunks


def around_fit(x, n_fit):
    return [x] + [lax.ppermute(x, "fit", shifted(n_fit, d)) for d in range(1, n_fit)]


def per_device(blocks, occ_energy, pair_list, pno_sizes, fock_virt):
    n = lax.axis_size("orb")
    n_fit = lax.axis_size("fit")
    n_rep = lax.axis_size("rep")
    local_orbs, fit_rows, virt = blocks.shape
    total_orbs = local_orbs * n
    me = lax.axis_index("orb")

    far_blocks = pltpu.with_memory_space_constraint(blocks, pltpu.HBM)
    endpoints = pair_list.reshape(-1)
    relative = (endpoints - me * local_orbs) % total_orbs
    named = jnp.any(
        relative[:, None] == jnp.arange(total_orbs, dtype=jnp.int32)[None, :], axis=0
    ).reshape(n, local_orbs)
    table = named.astype(jnp.int32)
    position = jnp.cumsum(table, axis=1) - 1
    columns = jnp.arange(CAP, dtype=jnp.int32)
    locals_ = jnp.arange(local_orbs, dtype=jnp.int32)
    matches = table[:, :, None] * (position[:, :, None] == columns[None, None, :])
    wanted = jnp.sum(matches * locals_[None, :, None], axis=1)
    end_hot = relative[:, None] == jnp.arange(total_orbs, dtype=jnp.int32)[None, :]
    slots = (relative // local_orbs) * CAP + jnp.sum(
        jnp.where(end_hot, position.reshape(1, -1), 0), axis=1
    )
    slots = slots.astype(jnp.int32)

    energies_here = occ_energy.astype(F32)
    got = {}
    for d in range(1, n):
        note = jnp.concatenate([wanted[d].astype(F32), energies_here])
        got[d] = lax.ppermute(note, "orb", shifted(n, d))
    asked = jnp.stack(
        [wanted[0]] + [got[d][:CAP].astype(jnp.int32) for d in range(1, n)]
    )
    energies = jnp.concatenate([energies_here] + [got[n - d][CAP:] for d in range(1, n)])

    chunks = cut_rows(fit_rows, FORWARD_ROWS)
    fit = lax.axis_index("fit").astype(jnp.int32).reshape(1)
    mine = around_fit(pick_blocks(wanted[:1], far_blocks, 0, fit_rows)[0], n_fit)
    inverse, off = prepare_pairs(energies, relative, pno_sizes, fock_virt)
    merged, arrived = [], []
    ints = None

    def pass_on(place, after):
        merged.append(around_fit(merge_chunk(arrived[place], after), n_fit))

    def integrals(place, before, after):
        here = slice(place, place + 1)
        return exchange_chunks(slots, fit, chunks[here], mine, merged[here], before, after)

    count = len(chunks)
    early = count - MIDDLE_CHUNKS
    for place in range(count + 1):
        if place < count:
            c = chunks[place]
            after = [mine[0]] if place < 2 else [merged[place - 2][0]]
            source = far_blocks if place == 0 else blocks
            picked = pick_blocks(asked[1:], source, c.start, c.count, after)
            arrived.append(
                [lax.ppermute(picked[d - 1], "orb", shifted(n, n - d)) for d in range(1, n)]
            )
        if place > 0:
            after = [picked[0]] if place < count else []
            after += [inverse] if place == PREPARE_AT else []
            after += [arrived[1][j] for j in FIRST_WAITS] if place == 1 else []
            after += merged[-1][1:] if place > SWAP_FIRST else []
            done = place - 1 - INTEGRAL_LAG
            if 0 <= done < early:
                ints = integrals(done, ints, [])
                after.append(ints)
            pass_on(place - 1, after)
    for place in range(max(count - INTEGRAL_LAG, 0), early):
        ints = integrals(place, ints, [merged[-1][0]])
    amplitudes, weights, *sums = middle_step(
        slots, fit, chunks[early:], mine, merged[early:], ints, inverse, off
    )

    first = chunks[-1]
    back = [(first, sums)]
    for c in reversed(cut_rows(first.start, BACK_ROWS)):
        parts, sources = [], []
        for place, chunk in enumerate(chunks[:-1]):
            low = max(c.start, chunk.start)
            high = min(c.start + c.count, chunk.start + chunk.count)
            if low < high:
                parts.append((low, low - chunk.start, high - low))
                sources.append(merged[place][0])
        after = back[-1][1][:1] if CHAIN_GRADIENTS else []
        back.append((c, gradient_chunk(slots, weights, mine[0], parts, sources, after)))

    swap = shifted(n_rep, 1)
    waiting = []
    returned = [
        [sums[0]] + [lax.ppermute(sums[d], "orb", shifted(n, d)) for d in range(1, n)]
        for _, sums in back
    ]
    low = 0
    for high in BACK_GROUPS:
        after = [w[1] for w in waiting[-1:]]
        if high == len(back):
            after = [w[2] for w in waiting[SETTLE_FROM:]]
        here = settle_chunks(asked, returned[low:high], local_orbs, after)
        group = [c for c, _ in back[low:high]]
        waiting.append((group, here, lax.ppermute(here, "rep", swap)))
        low = high
    grads = add_chunks(waiting[:-1], fit_rows)
    grads = add_chunks(waiting[-1:], fit_rows, grads)
    return amplitudes, grads


def solution(mesh):
    placed = (
        P(("groups", "orb"), "fit", None),
        P(("groups", "orb")),
        P(("groups", "orb", "rep"), None),
        P(("groups", "orb", "rep")),
        P(("groups", "orb", "rep"), None, None),
    )
    return jax.shard_map(
        per_device,
        mesh=mesh,
        in_specs=placed,
        out_specs=(P(("groups", "orb", "rep"), None, None), P(("groups", "orb"), "fit", None)),
        check_vma=False,
    )
```

```python
import functools
from typing import NamedTuple

import jax
import jax.numpy as jnp
from jax import lax
from jax.experimental import pallas as pl
from jax.experimental.pallas import tpu as pltpu
from jax.sharding import PartitionSpec as P

CAP = 2
FORWARD_ROWS = (16, 13, 10, 9, 8, 8)
MIDDLE_CHUNKS = 2
INTEGRAL_LAG = 3
BACK_ROWS = (14, 14, 15, 15)
BACK_GROUPS = (2, 3, 4, 5)
CHAIN_GRADIENTS = False
SETTLE_FROM = 99
UNROLL = 4
PREPARE_AT = 1
FIRST_WAITS = (2,)
SETTLE_WEIGHT = 50
MERGE_WEIGHT = 50
EXCHANGE_WEIGHT = 50
PICK_WEIGHT = 1
PREPARE_WEIGHT = 1
SWAP_FIRST = 9
VMEM_LIMIT = 40 * 1024 * 1024

F32 = jnp.float32
BF16 = jnp.bfloat16

ANY = pl.BlockSpec(memory_space=pl.ANY)
SMEM = pl.BlockSpec(memory_space=pltpu.SMEM)
VMEM = pl.BlockSpec(memory_space=pltpu.VMEM)


def params():
    return pltpu.CompilerParams(vmem_limit_bytes=VMEM_LIMIT)


def cost(flops, nbytes):
    return pl.CostEstimate(flops=int(flops), bytes_accessed=int(nbytes), transcendentals=0)


def weighed(times, flops, nbytes):
    return cost(times * flops, times * nbytes)


def shifted(n, d):
    return [(s, (s + d) % n) for s in range(n)]


def pick_kernel(start, rows, waits, index_ref, blocks_ref, *rest):
    outs, sems = rest[waits:-1], rest[-1]
    copies = []
    for d, out in enumerate(outs):
        for k in range(CAP):
            copies.append(
                pltpu.make_async_copy(
                    blocks_ref.at[index_ref[d, k], pl.ds(start, rows)],
                    out.at[k],
                    sems.at[d * CAP + k],
                )
            )
    for c in copies:
        c.start()
    for c in copies:
        c.wait()


def pick_blocks(index, blocks, start, rows, after=()):
    count = index.shape[0]
    virt = blocks.shape[2]
    shape = jax.ShapeDtypeStruct((CAP, rows, virt), BF16)
    return pl.pallas_call(
        functools.partial(pick_kernel, start, rows, len(after)),
        out_shape=[shape] * count,
        in_specs=[SMEM, ANY] + [ANY] * len(after),
        out_specs=[ANY] * count,
        scratch_shapes=[pltpu.SemaphoreType.DMA((count * CAP,))],
        compiler_params=params(),
        cost_estimate=weighed(PICK_WEIGHT, 0, 2 * count * CAP * rows * virt * 2),
        name="pick_blocks",
    )(index, blocks, *after)


def merge_kernel(count, *refs):
    sources, out, sems = refs[:count], refs[-2], refs[-1]
    copies = [
        pltpu.make_async_copy(ref, out.at[pl.ds(d * CAP, CAP)], sems.at[d])
        for d, ref in enumerate(sources)
    ]
    for c in copies:
        c.start()
    for c in copies:
        c.wait()


def merge_chunk(arrived, after=()):
    count = len(arrived)
    _, rows, virt = arrived[0].shape
    return pl.pallas_call(
        functools.partial(merge_kernel, count),
        out_shape=jax.ShapeDtypeStruct((count * CAP, rows, virt), BF16),
        in_specs=[ANY] * (count + len(after)),
        out_specs=ANY,
        scratch_shapes=[pltpu.SemaphoreType.DMA((count,))],
        compiler_params=params(),
        cost_estimate=weighed(MERGE_WEIGHT, 0, 4 * count * CAP * rows * virt),
        name="merge_chunk",
    )(*arrived, *after)


class Rows(NamedTuple):
    start: int
    count: int


def load_all(fit_ref, chunks, mine, merged, held, sems):
    n_fit = len(mine)
    total = sum(c.count for c in chunks)
    copies = []
    for f in range(n_fit):
        place = lax.rem(fit_ref[0] + (n_fit - f), n_fit)
        at = 0
        for i, c in enumerate(chunks):
            rows = pl.ds(pl.multiple_of(place * total + at, 16), c.count)
            copies.append(
                pltpu.make_async_copy(
                    mine[f].at[:, pl.ds(c.start, c.count)],
                    held.at[pl.ds(0, CAP), rows],
                    sems.at[len(copies)],
                )
            )
            copies.append(
                pltpu.make_async_copy(
                    merged[i][f],
                    held.at[pl.ds(CAP, held.shape[0] - CAP), rows],
                    sems.at[len(copies)],
                )
            )
            at += c.count
    for c in copies:
        c.start()
    return copies


def cross(left, right):
    return lax.dot_general(left, right, (((0,), (0,)), ((), ())), preferred_element_type=F32)


def split_refs(rest, n_fit, chunks):
    mine, rest = rest[:n_fit], rest[n_fit:]
    merged = []
    for _ in chunks:
        merged.append(rest[:n_fit])
        rest = rest[n_fit:]
    return mine, merged, rest


def exchange_kernel(chunks, n_fit, first, waits, slot_ref, fit_ref, *rest):
    mine, merged, rest = split_refs(rest[waits:], n_fit, chunks)
    if not first:
        before_ref, rest = rest[0], rest[1:]
    out_ref, held, sems = rest
    for c in load_all(fit_ref, chunks, mine, merged, held, sems):
        c.wait()

    def step(p, carry):
        product = cross(held[slot_ref[2 * p]], held[slot_ref[2 * p + 1]])
        if not first:
            product = before_ref[p] + product
        out_ref[p] = product
        return carry

    lax.fori_loop(0, out_ref.shape[0], step, 0)


def exchange_chunks(slots, fit, chunks, mine, merged, before, after=()):
    n_fit = len(mine)
    pairs = slots.shape[0] // 2
    virt = mine[0].shape[2]
    all_slots = CAP + merged[0][0].shape[0]
    rows = sum(c.count for c in chunks) * n_fit
    first = before is None
    return pl.pallas_call(
        functools.partial(exchange_kernel, chunks, n_fit, first, len(after)),
        out_shape=jax.ShapeDtypeStruct((pairs, virt, virt), F32),
        in_specs=[SMEM, SMEM]
        + [ANY] * (len(after) + n_fit * (1 + len(chunks)))
        + ([] if first else [VMEM]),
        out_specs=VMEM,
        scratch_shapes=[
            pltpu.VMEM((all_slots, rows, virt), BF16),
            pltpu.SemaphoreType.DMA((2 * n_fit * len(chunks),)),
        ],
        compiler_params=params(),
        cost_estimate=weighed(EXCHANGE_WEIGHT,
            2 * pairs * rows * virt * virt, all_slots * rows * virt * 2 + pairs * virt * virt * 8
        ),
        name="exchange_chunks",
    )(slots, fit, *after, *mine, *[x for m in merged for x in m], *([] if first else [before]))


def prepare_kernel(energy_ref, ends_ref, size_ref, fock_ref, inverse_ref, off_ref):
    p = pl.program_id(0)
    virt = fock_ref.shape[-1]
    occ = energy_ref[ends_ref[2 * p]] + energy_ref[ends_ref[2 * p + 1]]
    size = size_ref[p]
    fock = fock_ref[0]
    row = lax.broadcasted_iota(jnp.int32, (virt, virt), 0)
    col = lax.broadcasted_iota(jnp.int32, (virt, virt), 1)
    on_diagonal = row == col
    diagonal = jnp.where(on_diagonal, fock, 0.0)
    denominator = (
        jnp.sum(diagonal, axis=1, keepdims=True) + jnp.sum(diagonal, axis=0, keepdims=True) - occ
    )
    inverse_ref[0] = jnp.where((row < size) & (col < size), 1.0 / denominator, 0.0)
    off_ref[0] = jnp.where(on_diagonal, 0.0, fock).astype(BF16)


def prepare_pairs(energies, ends, sizes, fock):
    pairs, virt, _ = fock.shape
    block = pl.BlockSpec((1, virt, virt), lambda p: (p, 0, 0))
    return pl.pallas_call(
        prepare_kernel,
        grid=(pairs,),
        out_shape=[
            jax.ShapeDtypeStruct((pairs, virt, virt), F32),
            jax.ShapeDtypeStruct((pairs, virt, virt), BF16),
        ],
        in_specs=[SMEM, SMEM, SMEM, block],
        out_specs=[block, block],
        compiler_params=params(),
        cost_estimate=weighed(PREPARE_WEIGHT, 10 * pairs * virt * virt, pairs * virt * virt * 10),
        name="prepare_pairs",
    )(energies, ends, sizes, fock)


def add_gradients(slot_ref, weight_ref, block_of, sums, outs):
    sums[...] = jnp.zeros_like(sums)

    def step(p, carry):
        left = slot_ref[2 * p]
        right = slot_ref[2 * p + 1]
        sums[left] += jnp.dot(block_of(right), weight_ref[2 * p], preferred_element_type=F32)
        sums[right] += jnp.dot(block_of(left), weight_ref[2 * p + 1], preferred_element_type=F32)
        return carry

    lax.fori_loop(0, weight_ref.shape[0] // 2, step, 0)
    for d, out in enumerate(outs):
        for k in range(CAP):
            out[k] = sums[d * CAP + k].astype(BF16)


def middle_kernel(chunks, n, n_fit, slot_ref, fit_ref, *rest):
    mine, merged, rest = split_refs(rest, n_fit, chunks)
    before_ref, inverse_ref, off_ref, amp_ref, weight_ref = rest[:5]
    outs = rest[5 : 5 + n]
    held, sums, sems = rest[5 + n :]
    for c in load_all(fit_ref, chunks, mine, merged, held, sems):
        c.wait()

    def step(p, carry):
        total = before_ref[p] + cross(held[slot_ref[2 * p]], held[slot_ref[2 * p + 1]])
        inverse = inverse_ref[p]
        off = off_ref[p]
        current = -total * inverse
        rounded = current.astype(BF16)
        change = jnp.dot(off, rounded, preferred_element_type=F32) + jnp.dot(
            rounded, off, preferred_element_type=F32
        )
        amp = (current - change * inverse).astype(BF16)
        amp_ref[p] = amp
        wide = amp.astype(F32)
        flipped = wide.T
        weight_ref[2 * p] = (2.0 * flipped - wide).astype(BF16)
        weight_ref[2 * p + 1] = (2.0 * wide - flipped).astype(BF16)
        return carry

    lax.fori_loop(0, amp_ref.shape[0], step, 0, unroll=UNROLL)
    total = sum(c.count for c in chunks)
    last = chunks[-1].count
    here = pl.ds(pl.multiple_of(fit_ref[0] * total + total - last, 16), last)
    add_gradients(slot_ref, weight_ref, lambda s: held[s, here], sums, outs)


def middle_step(slots, fit, chunks, mine, merged, before, inverse, off):
    n_fit = len(mine)
    pairs, virt, _ = before.shape
    all_slots = CAP + merged[0][0].shape[0]
    n = all_slots // CAP
    rows = sum(c.count for c in chunks)
    return pl.pallas_call(
        functools.partial(middle_kernel, chunks, n, n_fit),
        out_shape=[
            jax.ShapeDtypeStruct((pairs, virt, virt), BF16),
            jax.ShapeDtypeStruct((2 * pairs, virt, virt), BF16),
        ]
        + [jax.ShapeDtypeStruct((CAP, chunks[-1].count, virt), BF16)] * n,
        in_specs=[SMEM, SMEM] + [ANY] * (n_fit * (1 + len(chunks))) + [VMEM] * 3,
        out_specs=[VMEM] * (2 + n),
        scratch_shapes=[
            pltpu.VMEM((all_slots, n_fit * rows, virt), BF16),
            pltpu.VMEM((all_slots, chunks[-1].count, virt), F32),
            pltpu.SemaphoreType.DMA((2 * n_fit * len(chunks),)),
        ],
        compiler_params=params(),
        cost_estimate=cost(
            pairs * (4 * virt**3 + 6 * rows * n_fit * virt * virt), pairs * virt * virt * 16
        ),
        name="middle_step",
    )(slots, fit, *mine, *[x for m in merged for x in m], before, inverse, off)


def gradient_kernel(parts, n, slot_ref, weight_ref, mine_ref, *rest):
    merged = rest[: len(parts)]
    held, sums, sems = rest[-3:]
    outs = rest[-3 - n : -3]
    copies = []
    at = 0
    for (start, offset, rows), ref in zip(parts, merged):
        to = pl.ds(at, rows)
        copies.append(
            pltpu.make_async_copy(
                mine_ref.at[:, pl.ds(start, rows)],
                held.at[pl.ds(0, CAP), to],
                sems.at[len(copies)],
            )
        )
        copies.append(
            pltpu.make_async_copy(
                ref.at[:, pl.ds(offset, rows)],
                held.at[pl.ds(CAP, held.shape[0] - CAP), to],
                sems.at[len(copies)],
            )
        )
        at += rows
    for c in copies:
        c.start()
    for c in copies:
        c.wait()
    add_gradients(slot_ref, weight_ref, lambda s: held[s], sums, outs)


def gradient_chunk(slots, weights, mine, parts, merged, after):
    ends = slots.shape[0]
    virt = mine.shape[2]
    all_slots = CAP + merged[0].shape[0]
    n = all_slots // CAP
    rows = sum(p[2] for p in parts)
    return pl.pallas_call(
        functools.partial(gradient_kernel, parts, n),
        out_shape=[jax.ShapeDtypeStruct((CAP, rows, virt), BF16)] * n,
        in_specs=[SMEM, VMEM, ANY] + [ANY] * (len(parts) + len(after)),
        out_specs=[VMEM] * n,
        scratch_shapes=[
            pltpu.VMEM((all_slots, rows, virt), BF16),
            pltpu.VMEM((all_slots, rows, virt), F32),
            pltpu.SemaphoreType.DMA((2 * len(parts),)),
        ],
        compiler_params=params(),
        cost_estimate=cost(
            2 * ends * rows * virt * virt, 4 * all_slots * rows * virt + ends * virt * virt * 2
        ),
        name="gradient_chunk",
    )(slots, weights, mine, *merged, *after)


def settle_kernel(shape, index_ref, *rest):
    out_ref, sums = rest[-2:]
    sums[...] = jnp.zeros_like(sums)
    at = 0
    for count in shape:
        rows = pl.ds(at, rest[0].shape[1])
        at += rest[0].shape[1]
        for d, ref in enumerate(rest[:count]):
            for k in range(CAP):
                g = index_ref[d, k]
                sums[g, rows] += ref[k].astype(F32)
        rest = rest[count:]
    out_ref[...] = sums[...].astype(BF16)


def settle_chunks(index, returned, local_orbs, after=()):
    rows = sum(r[0].shape[1] for r in returned)
    virt = returned[0][0].shape[2]
    terms = [x for r in returned for x in r]
    return pl.pallas_call(
        functools.partial(settle_kernel, [len(r) for r in returned]),
        out_shape=jax.ShapeDtypeStruct((local_orbs, rows, virt), BF16),
        in_specs=[SMEM] + [VMEM] * len(terms) + [ANY] * len(after),
        out_specs=VMEM,
        scratch_shapes=[pltpu.VMEM((local_orbs, rows, virt), F32)],
        compiler_params=params(),
        cost_estimate=weighed(SETTLE_WEIGHT, 0, (len(returned[0]) * CAP + local_orbs) * 2 * rows * virt),
        name="settle_chunks",
    )(index, *terms, *after)


def add_kernel(groups, *refs):
    count = len(groups)
    grads_ref, wide, sems = refs[-3:]
    copies = []
    at = 0
    for i, group in enumerate(groups):
        mine, other = refs[i], refs[count + i]
        offset = 0
        for c in group:
            rows, source = pl.ds(at, c.count), pl.ds(offset, c.count)
            at, offset = at + c.count, offset + c.count
            for g in range(mine.shape[0]):
                wide[g, rows] = mine[g, source].astype(F32) + other[g, source].astype(F32)
                copies.append(
                    pltpu.make_async_copy(
                        wide.at[g, rows],
                        grads_ref.at[g, pl.ds(c.start, c.count)],
                        sems.at[len(copies)],
                    )
                )
                copies[-1].start()
    for c in copies:
        c.wait()


def add_chunks(waiting, fit_rows, grads=None):
    groups, mine, other = zip(*waiting)
    local_orbs, _, virt = mine[0].shape
    rows = sum(m.shape[1] for m in mine)
    count = len(mine)
    more = [] if grads is None else [grads]
    return pl.pallas_call(
        functools.partial(add_kernel, groups),
        out_shape=jax.ShapeDtypeStruct((local_orbs, fit_rows, virt), F32),
        in_specs=[VMEM] * (2 * count) + [ANY] * len(more),
        out_specs=ANY,
        scratch_shapes=[
            pltpu.VMEM((local_orbs, rows, virt), F32),
            pltpu.SemaphoreType.DMA((local_orbs * sum(len(g) for g in groups),)),
        ],
        input_output_aliases={} if grads is None else {2 * count: 0},
        compiler_params=params(),
        cost_estimate=cost(0, 8 * local_orbs * rows * virt),
        name="add_chunks",
    )(*mine, *other, *more)


def cut_rows(total, weights):
    unit = 16
    units = total // unit
    whole = sum(weights)
    sizes = [max(1, units * w // whole) for w in weights]
    sizes[0] += units - sum(sizes)
    chunks, at = [], 0
    for size in sizes:
        chunks.append(Rows(at, size * unit))
        at += size * unit
    return chunks


def around_fit(x, n_fit):
    return [x] + [lax.ppermute(x, "fit", shifted(n_fit, d)) for d in range(1, n_fit)]


def per_device(blocks, occ_energy, pair_list, pno_sizes, fock_virt):
    n = lax.axis_size("orb")
    n_fit = lax.axis_size("fit")
    n_rep = lax.axis_size("rep")
    local_orbs, fit_rows, virt = blocks.shape
    total_orbs = local_orbs * n
    me = lax.axis_index("orb")

    far_blocks = pltpu.with_memory_space_constraint(blocks, pltpu.HBM)
    endpoints = pair_list.reshape(-1)
    relative = (endpoints - me * local_orbs) % total_orbs
    named = jnp.any(
        relative[:, None] == jnp.arange(total_orbs, dtype=jnp.int32)[None, :], axis=0
    ).reshape(n, local_orbs)
    table = named.astype(jnp.int32)
    position = jnp.cumsum(table, axis=1) - 1
    columns = jnp.arange(CAP, dtype=jnp.int32)
    locals_ = jnp.arange(local_orbs, dtype=jnp.int32)
    matches = table[:, :, None] * (position[:, :, None] == columns[None, None, :])
    wanted = jnp.sum(matches * locals_[None, :, None], axis=1)
    end_hot = relative[:, None] == jnp.arange(total_orbs, dtype=jnp.int32)[None, :]
    slots = (relative // local_orbs) * CAP + jnp.sum(
        jnp.where(end_hot, position.reshape(1, -1), 0), axis=1
    )
    slots = slots.astype(jnp.int32)

    energies_here = occ_energy.astype(F32)
    got = {}
    for d in range(1, n):
        note = jnp.concatenate([wanted[d].astype(F32), energies_here])
        got[d] = lax.ppermute(note, "orb", shifted(n, d))
    asked = jnp.stack(
        [wanted[0]] + [got[d][:CAP].astype(jnp.int32) for d in range(1, n)]
    )
    energies = jnp.concatenate([energies_here] + [got[n - d][CAP:] for d in range(1, n)])

    chunks = cut_rows(fit_rows, FORWARD_ROWS)
    fit = lax.axis_index("fit").astype(jnp.int32).reshape(1)
    mine = around_fit(pick_blocks(wanted[:1], far_blocks, 0, fit_rows)[0], n_fit)
    inverse, off = prepare_pairs(energies, relative, pno_sizes, fock_virt)
    merged, arrived = [], []
    ints = None

    def pass_on(place, after):
        merged.append(around_fit(merge_chunk(arrived[place], after), n_fit))

    def integrals(place, before, after):
        here = slice(place, place + 1)
        return exchange_chunks(slots, fit, chunks[here], mine, merged[here], before, after)

    count = len(chunks)
    early = count - MIDDLE_CHUNKS
    for place in range(count + 1):
        if place < count:
            c = chunks[place]
            after = [mine[0]] if place < 2 else [merged[place - 2][0]]
            source = far_blocks if place == 0 else blocks
            picked = pick_blocks(asked[1:], source, c.start, c.count, after)
            arrived.append(
                [lax.ppermute(picked[d - 1], "orb", shifted(n, n - d)) for d in range(1, n)]
            )
        if place > 0:
            after = [picked[0]] if place < count else []
            after += [inverse] if place == PREPARE_AT else []
            after += [arrived[1][j] for j in FIRST_WAITS] if place == 1 else []
            after += merged[-1][1:] if place > SWAP_FIRST else []
            done = place - 1 - INTEGRAL_LAG
            if 0 <= done < early:
                ints = integrals(done, ints, [])
                after.append(ints)
            pass_on(place - 1, after)
    for place in range(max(count - INTEGRAL_LAG, 0), early):
        ints = integrals(place, ints, [merged[-1][0]])
    amplitudes, weights, *sums = middle_step(
        slots, fit, chunks[early:], mine, merged[early:], ints, inverse, off
    )

    first = chunks[-1]
    back = [(first, sums)]
    for c in reversed(cut_rows(first.start, BACK_ROWS)):
        parts, sources = [], []
        for place, chunk in enumerate(chunks[:-1]):
            low = max(c.start, chunk.start)
            high = min(c.start + c.count, chunk.start + chunk.count)
            if low < high:
                parts.append((low, low - chunk.start, high - low))
                sources.append(merged[place][0])
        after = back[-1][1][:1] if CHAIN_GRADIENTS else []
        back.append((c, gradient_chunk(slots, weights, mine[0], parts, sources, after)))

    swap = shifted(n_rep, 1)
    waiting = []
    returned = [
        [sums[0]] + [lax.ppermute(sums[d], "orb", shifted(n, d)) for d in range(1, n)]
        for _, sums in back
    ]
    low = 0
    for high in BACK_GROUPS:
        after = [w[1] for w in waiting[-1:]]
        if high == len(back):
            after = [w[2] for w in waiting[SETTLE_FROM:]]
        here = settle_chunks(asked, returned[low:high], local_orbs, after)
        group = [c for c, _ in back[low:high]]
        waiting.append((group, here, lax.ppermute(here, "rep", swap)))
        low = high
    grads = add_chunks(waiting[:-1], fit_rows)
    grads = add_chunks(waiting[-1:], fit_rows, grads)
    return amplitudes, grads


def solution(mesh):
    placed = (
        P(("groups", "orb"), "fit", None),
        P(("groups", "orb")),
        P(("groups", "orb", "rep"), None),
        P(("groups", "orb", "rep")),
        P(("groups", "orb", "rep"), None, None),
    )
    return jax.shard_map(
        per_device,
        mesh=mesh,
        in_specs=placed,
        out_specs=(P(("groups", "orb", "rep"), None, None), P(("groups", "orb"), "fit", None)),
        check_vma=False,
    )
```

```python
import functools
from typing import NamedTuple

import jax
import jax.numpy as jnp
from jax import lax
from jax.experimental import pallas as pl
from jax.experimental.pallas import tpu as pltpu
from jax.sharding import PartitionSpec as P

CAP = 2
FORWARD_ROWS = (16, 13, 10, 9, 8, 8)
MIDDLE_CHUNKS = 2
INTEGRAL_LAG = 3
BACK_ROWS = (14, 14, 15, 15)
BACK_GROUPS = (2, 3, 4, 5)
CHAIN_GRADIENTS = False
SETTLE_FROM = 99
UNROLL = 8
PREPARE_AT = 1
FIRST_WAITS = (2,)
SETTLE_WEIGHT = 50
MERGE_WEIGHT = 50
EXCHANGE_WEIGHT = 50
PICK_WEIGHT = 1
PREPARE_WEIGHT = 1
SWAP_FIRST = 9
VMEM_LIMIT = 40 * 1024 * 1024

F32 = jnp.float32
BF16 = jnp.bfloat16

ANY = pl.BlockSpec(memory_space=pl.ANY)
SMEM = pl.BlockSpec(memory_space=pltpu.SMEM)
VMEM = pl.BlockSpec(memory_space=pltpu.VMEM)


def params():
    return pltpu.CompilerParams(vmem_limit_bytes=VMEM_LIMIT)


def cost(flops, nbytes):
    return pl.CostEstimate(flops=int(flops), bytes_accessed=int(nbytes), transcendentals=0)


def weighed(times, flops, nbytes):
    return cost(times * flops, times * nbytes)


def shifted(n, d):
    return [(s, (s + d) % n) for s in range(n)]


def pick_kernel(start, rows, waits, index_ref, blocks_ref, *rest):
    outs, sems = rest[waits:-1], rest[-1]
    copies = []
    for d, out in enumerate(outs):
        for k in range(CAP):
            copies.append(
                pltpu.make_async_copy(
                    blocks_ref.at[index_ref[d, k], pl.ds(start, rows)],
                    out.at[k],
                    sems.at[d * CAP + k],
                )
            )
    for c in copies:
        c.start()
    for c in copies:
        c.wait()


def pick_blocks(index, blocks, start, rows, after=()):
    count = index.shape[0]
    virt = blocks.shape[2]
    shape = jax.ShapeDtypeStruct((CAP, rows, virt), BF16)
    return pl.pallas_call(
        functools.partial(pick_kernel, start, rows, len(after)),
        out_shape=[shape] * count,
        in_specs=[SMEM, ANY] + [ANY] * len(after),
        out_specs=[ANY] * count,
        scratch_shapes=[pltpu.SemaphoreType.DMA((count * CAP,))],
        compiler_params=params(),
        cost_estimate=weighed(PICK_WEIGHT, 0, 2 * count * CAP * rows * virt * 2),
        name="pick_blocks",
    )(index, blocks, *after)


def merge_kernel(count, *refs):
    sources, out, sems = refs[:count], refs[-2], refs[-1]
    copies = [
        pltpu.make_async_copy(ref, out.at[pl.ds(d * CAP, CAP)], sems.at[d])
        for d, ref in enumerate(sources)
    ]
    for c in copies:
        c.start()
    for c in copies:
        c.wait()


def merge_chunk(arrived, after=()):
    count = len(arrived)
    _, rows, virt = arrived[0].shape
    return pl.pallas_call(
        functools.partial(merge_kernel, count),
        out_shape=jax.ShapeDtypeStruct((count * CAP, rows, virt), BF16),
        in_specs=[ANY] * (count + len(after)),
        out_specs=ANY,
        scratch_shapes=[pltpu.SemaphoreType.DMA((count,))],
        compiler_params=params(),
        cost_estimate=weighed(MERGE_WEIGHT, 0, 4 * count * CAP * rows * virt),
        name="merge_chunk",
    )(*arrived, *after)


class Rows(NamedTuple):
    start: int
    count: int


def load_all(fit_ref, chunks, mine, merged, held, sems):
    n_fit = len(mine)
    total = sum(c.count for c in chunks)
    copies = []
    for f in range(n_fit):
        place = lax.rem(fit_ref[0] + (n_fit - f), n_fit)
        at = 0
        for i, c in enumerate(chunks):
            rows = pl.ds(pl.multiple_of(place * total + at, 16), c.count)
            copies.append(
                pltpu.make_async_copy(
                    mine[f].at[:, pl.ds(c.start, c.count)],
                    held.at[pl.ds(0, CAP), rows],
                    sems.at[len(copies)],
                )
            )
            copies.append(
                pltpu.make_async_copy(
                    merged[i][f],
                    held.at[pl.ds(CAP, held.shape[0] - CAP), rows],
                    sems.at[len(copies)],
                )
            )
            at += c.count
    for c in copies:
        c.start()
    return copies


def cross(left, right):
    return lax.dot_general(left, right, (((0,), (0,)), ((), ())), preferred_element_type=F32)


def split_refs(rest, n_fit, chunks):
    mine, rest = rest[:n_fit], rest[n_fit:]
    merged = []
    for _ in chunks:
        merged.append(rest[:n_fit])
        rest = rest[n_fit:]
    return mine, merged, rest


def exchange_kernel(chunks, n_fit, first, waits, slot_ref, fit_ref, *rest):
    mine, merged, rest = split_refs(rest[waits:], n_fit, chunks)
    if not first:
        before_ref, rest = rest[0], rest[1:]
    out_ref, held, sems = rest
    for c in load_all(fit_ref, chunks, mine, merged, held, sems):
        c.wait()

    def step(p, carry):
        product = cross(held[slot_ref[2 * p]], held[slot_ref[2 * p + 1]])
        if not first:
            product = before_ref[p] + product
        out_ref[p] = product
        return carry

    lax.fori_loop(0, out_ref.shape[0], step, 0)


def exchange_chunks(slots, fit, chunks, mine, merged, before, after=()):
    n_fit = len(mine)
    pairs = slots.shape[0] // 2
    virt = mine[0].shape[2]
    all_slots = CAP + merged[0][0].shape[0]
    rows = sum(c.count for c in chunks) * n_fit
    first = before is None
    return pl.pallas_call(
        functools.partial(exchange_kernel, chunks, n_fit, first, len(after)),
        out_shape=jax.ShapeDtypeStruct((pairs, virt, virt), F32),
        in_specs=[SMEM, SMEM]
        + [ANY] * (len(after) + n_fit * (1 + len(chunks)))
        + ([] if first else [VMEM]),
        out_specs=VMEM,
        scratch_shapes=[
            pltpu.VMEM((all_slots, rows, virt), BF16),
            pltpu.SemaphoreType.DMA((2 * n_fit * len(chunks),)),
        ],
        compiler_params=params(),
        cost_estimate=weighed(EXCHANGE_WEIGHT,
            2 * pairs * rows * virt * virt, all_slots * rows * virt * 2 + pairs * virt * virt * 8
        ),
        name="exchange_chunks",
    )(slots, fit, *after, *mine, *[x for m in merged for x in m], *([] if first else [before]))


def prepare_kernel(energy_ref, ends_ref, size_ref, fock_ref, inverse_ref, off_ref):
    p = pl.program_id(0)
    virt = fock_ref.shape[-1]
    occ = energy_ref[ends_ref[2 * p]] + energy_ref[ends_ref[2 * p + 1]]
    size = size_ref[p]
    fock = fock_ref[0]
    row = lax.broadcasted_iota(jnp.int32, (virt, virt), 0)
    col = lax.broadcasted_iota(jnp.int32, (virt, virt), 1)
    on_diagonal = row == col
    diagonal = jnp.where(on_diagonal, fock, 0.0)
    denominator = (
        jnp.sum(diagonal, axis=1, keepdims=True) + jnp.sum(diagonal, axis=0, keepdims=True) - occ
    )
    inverse_ref[0] = jnp.where((row < size) & (col < size), 1.0 / denominator, 0.0)
    off_ref[0] = jnp.where(on_diagonal, 0.0, fock).astype(BF16)


def prepare_pairs(energies, ends, sizes, fock):
    pairs, virt, _ = fock.shape
    block = pl.BlockSpec((1, virt, virt), lambda p: (p, 0, 0))
    return pl.pallas_call(
        prepare_kernel,
        grid=(pairs,),
        out_shape=[
            jax.ShapeDtypeStruct((pairs, virt, virt), F32),
            jax.ShapeDtypeStruct((pairs, virt, virt), BF16),
        ],
        in_specs=[SMEM, SMEM, SMEM, block],
        out_specs=[block, block],
        compiler_params=params(),
        cost_estimate=weighed(PREPARE_WEIGHT, 10 * pairs * virt * virt, pairs * virt * virt * 10),
        name="prepare_pairs",
    )(energies, ends, sizes, fock)


def add_gradients(slot_ref, weight_ref, block_of, sums, outs):
    sums[...] = jnp.zeros_like(sums)

    def step(p, carry):
        left = slot_ref[2 * p]
        right = slot_ref[2 * p + 1]
        sums[left] += jnp.dot(block_of(right), weight_ref[2 * p], preferred_element_type=F32)
        sums[right] += jnp.dot(block_of(left), weight_ref[2 * p + 1], preferred_element_type=F32)
        return carry

    lax.fori_loop(0, weight_ref.shape[0] // 2, step, 0)
    for d, out in enumerate(outs):
        for k in range(CAP):
            out[k] = sums[d * CAP + k].astype(BF16)


def middle_kernel(chunks, n, n_fit, slot_ref, fit_ref, *rest):
    mine, merged, rest = split_refs(rest, n_fit, chunks)
    before_ref, inverse_ref, off_ref, amp_ref, weight_ref = rest[:5]
    outs = rest[5 : 5 + n]
    held, sums, sems = rest[5 + n :]
    for c in load_all(fit_ref, chunks, mine, merged, held, sems):
        c.wait()

    def step(p, carry):
        total = before_ref[p] + cross(held[slot_ref[2 * p]], held[slot_ref[2 * p + 1]])
        inverse = inverse_ref[p]
        off = off_ref[p]
        current = -total * inverse
        rounded = current.astype(BF16)
        change = jnp.dot(off, rounded, preferred_element_type=F32) + jnp.dot(
            rounded, off, preferred_element_type=F32
        )
        amp = (current - change * inverse).astype(BF16)
        amp_ref[p] = amp
        wide = amp.astype(F32)
        flipped = wide.T
        weight_ref[2 * p] = (2.0 * flipped - wide).astype(BF16)
        weight_ref[2 * p + 1] = (2.0 * wide - flipped).astype(BF16)
        return carry

    lax.fori_loop(0, amp_ref.shape[0], step, 0, unroll=UNROLL)
    total = sum(c.count for c in chunks)
    last = chunks[-1].count
    here = pl.ds(pl.multiple_of(fit_ref[0] * total + total - last, 16), last)
    add_gradients(slot_ref, weight_ref, lambda s: held[s, here], sums, outs)


def middle_step(slots, fit, chunks, mine, merged, before, inverse, off):
    n_fit = len(mine)
    pairs, virt, _ = before.shape
    all_slots = CAP + merged[0][0].shape[0]
    n = all_slots // CAP
    rows = sum(c.count for c in chunks)
    return pl.pallas_call(
        functools.partial(middle_kernel, chunks, n, n_fit),
        out_shape=[
            jax.ShapeDtypeStruct((pairs, virt, virt), BF16),
            jax.ShapeDtypeStruct((2 * pairs, virt, virt), BF16),
        ]
        + [jax.ShapeDtypeStruct((CAP, chunks[-1].count, virt), BF16)] * n,
        in_specs=[SMEM, SMEM] + [ANY] * (n_fit * (1 + len(chunks))) + [VMEM] * 3,
        out_specs=[VMEM] * (2 + n),
        scratch_shapes=[
            pltpu.VMEM((all_slots, n_fit * rows, virt), BF16),
            pltpu.VMEM((all_slots, chunks[-1].count, virt), F32),
            pltpu.SemaphoreType.DMA((2 * n_fit * len(chunks),)),
        ],
        compiler_params=params(),
        cost_estimate=cost(
            pairs * (4 * virt**3 + 6 * rows * n_fit * virt * virt), pairs * virt * virt * 16
        ),
        name="middle_step",
    )(slots, fit, *mine, *[x for m in merged for x in m], before, inverse, off)


def gradient_kernel(parts, n, slot_ref, weight_ref, mine_ref, *rest):
    merged = rest[: len(parts)]
    held, sums, sems = rest[-3:]
    outs = rest[-3 - n : -3]
    copies = []
    at = 0
    for (start, offset, rows), ref in zip(parts, merged):
        to = pl.ds(at, rows)
        copies.append(
            pltpu.make_async_copy(
                mine_ref.at[:, pl.ds(start, rows)],
                held.at[pl.ds(0, CAP), to],
                sems.at[len(copies)],
            )
        )
        copies.append(
            pltpu.make_async_copy(
                ref.at[:, pl.ds(offset, rows)],
                held.at[pl.ds(CAP, held.shape[0] - CAP), to],
                sems.at[len(copies)],
            )
        )
        at += rows
    for c in copies:
        c.start()
    for c in copies:
        c.wait()
    add_gradients(slot_ref, weight_ref, lambda s: held[s], sums, outs)


def gradient_chunk(slots, weights, mine, parts, merged, after):
    ends = slots.shape[0]
    virt = mine.shape[2]
    all_slots = CAP + merged[0].shape[0]
    n = all_slots // CAP
    rows = sum(p[2] for p in parts)
    return pl.pallas_call(
        functools.partial(gradient_kernel, parts, n),
        out_shape=[jax.ShapeDtypeStruct((CAP, rows, virt), BF16)] * n,
        in_specs=[SMEM, VMEM, ANY] + [ANY] * (len(parts) + len(after)),
        out_specs=[VMEM] * n,
        scratch_shapes=[
            pltpu.VMEM((all_slots, rows, virt), BF16),
            pltpu.VMEM((all_slots, rows, virt), F32),
            pltpu.SemaphoreType.DMA((2 * len(parts),)),
        ],
        compiler_params=params(),
        cost_estimate=cost(
            2 * ends * rows * virt * virt, 4 * all_slots * rows * virt + ends * virt * virt * 2
        ),
        name="gradient_chunk",
    )(slots, weights, mine, *merged, *after)


def settle_kernel(shape, index_ref, *rest):
    out_ref, sums = rest[-2:]
    sums[...] = jnp.zeros_like(sums)
    at = 0
    for count in shape:
        rows = pl.ds(at, rest[0].shape[1])
        at += rest[0].shape[1]
        for d, ref in enumerate(rest[:count]):
            for k in range(CAP):
                g = index_ref[d, k]
                sums[g, rows] += ref[k].astype(F32)
        rest = rest[count:]
    out_ref[...] = sums[...].astype(BF16)


def settle_chunks(index, returned, local_orbs, after=()):
    rows = sum(r[0].shape[1] for r in returned)
    virt = returned[0][0].shape[2]
    terms = [x for r in returned for x in r]
    return pl.pallas_call(
        functools.partial(settle_kernel, [len(r) for r in returned]),
        out_shape=jax.ShapeDtypeStruct((local_orbs, rows, virt), BF16),
        in_specs=[SMEM] + [VMEM] * len(terms) + [ANY] * len(after),
        out_specs=VMEM,
        scratch_shapes=[pltpu.VMEM((local_orbs, rows, virt), F32)],
        compiler_params=params(),
        cost_estimate=weighed(SETTLE_WEIGHT, 0, (len(returned[0]) * CAP + local_orbs) * 2 * rows * virt),
        name="settle_chunks",
    )(index, *terms, *after)


def add_kernel(groups, *refs):
    count = len(groups)
    grads_ref, wide, sems = refs[-3:]
    copies = []
    at = 0
    for i, group in enumerate(groups):
        mine, other = refs[i], refs[count + i]
        offset = 0
        for c in group:
            rows, source = pl.ds(at, c.count), pl.ds(offset, c.count)
            at, offset = at + c.count, offset + c.count
            for g in range(mine.shape[0]):
                wide[g, rows] = mine[g, source].astype(F32) + other[g, source].astype(F32)
                copies.append(
                    pltpu.make_async_copy(
                        wide.at[g, rows],
                        grads_ref.at[g, pl.ds(c.start, c.count)],
                        sems.at[len(copies)],
                    )
                )
                copies[-1].start()
    for c in copies:
        c.wait()


def add_chunks(waiting, fit_rows, grads=None):
    groups, mine, other = zip(*waiting)
    local_orbs, _, virt = mine[0].shape
    rows = sum(m.shape[1] for m in mine)
    count = len(mine)
    more = [] if grads is None else [grads]
    return pl.pallas_call(
        functools.partial(add_kernel, groups),
        out_shape=jax.ShapeDtypeStruct((local_orbs, fit_rows, virt), F32),
        in_specs=[VMEM] * (2 * count) + [ANY] * len(more),
        out_specs=ANY,
        scratch_shapes=[
            pltpu.VMEM((local_orbs, rows, virt), F32),
            pltpu.SemaphoreType.DMA((local_orbs * sum(len(g) for g in groups),)),
        ],
        input_output_aliases={} if grads is None else {2 * count: 0},
        compiler_params=params(),
        cost_estimate=cost(0, 8 * local_orbs * rows * virt),
        name="add_chunks",
    )(*mine, *other, *more)


def cut_rows(total, weights):
    unit = 16
    units = total // unit
    whole = sum(weights)
    sizes = [max(1, units * w // whole) for w in weights]
    sizes[0] += units - sum(sizes)
    chunks, at = [], 0
    for size in sizes:
        chunks.append(Rows(at, size * unit))
        at += size * unit
    return chunks


def around_fit(x, n_fit):
    return [x] + [lax.ppermute(x, "fit", shifted(n_fit, d)) for d in range(1, n_fit)]


def per_device(blocks, occ_energy, pair_list, pno_sizes, fock_virt):
    n = lax.axis_size("orb")
    n_fit = lax.axis_size("fit")
    n_rep = lax.axis_size("rep")
    local_orbs, fit_rows, virt = blocks.shape
    total_orbs = local_orbs * n
    me = lax.axis_index("orb")

    far_blocks = pltpu.with_memory_space_constraint(blocks, pltpu.HBM)
    endpoints = pair_list.reshape(-1)
    relative = (endpoints - me * local_orbs) % total_orbs
    named = jnp.any(
        relative[:, None] == jnp.arange(total_orbs, dtype=jnp.int32)[None, :], axis=0
    ).reshape(n, local_orbs)
    table = named.astype(jnp.int32)
    position = jnp.cumsum(table, axis=1) - 1
    columns = jnp.arange(CAP, dtype=jnp.int32)
    locals_ = jnp.arange(local_orbs, dtype=jnp.int32)
    matches = table[:, :, None] * (position[:, :, None] == columns[None, None, :])
    wanted = jnp.sum(matches * locals_[None, :, None], axis=1)
    end_hot = relative[:, None] == jnp.arange(total_orbs, dtype=jnp.int32)[None, :]
    slots = (relative // local_orbs) * CAP + jnp.sum(
        jnp.where(end_hot, position.reshape(1, -1), 0), axis=1
    )
    slots = slots.astype(jnp.int32)

    energies_here = occ_energy.astype(F32)
    got = {}
    for d in range(1, n):
        note = jnp.concatenate([wanted[d].astype(F32), energies_here])
        got[d] = lax.ppermute(note, "orb", shifted(n, d))
    asked = jnp.stack(
        [wanted[0]] + [got[d][:CAP].astype(jnp.int32) for d in range(1, n)]
    )
    energies = jnp.concatenate([energies_here] + [got[n - d][CAP:] for d in range(1, n)])

    chunks = cut_rows(fit_rows, FORWARD_ROWS)
    fit = lax.axis_index("fit").astype(jnp.int32).reshape(1)
    mine = around_fit(pick_blocks(wanted[:1], far_blocks, 0, fit_rows)[0], n_fit)
    inverse, off = prepare_pairs(energies, relative, pno_sizes, fock_virt)
    merged, arrived = [], []
    ints = None

    def pass_on(place, after):
        merged.append(around_fit(merge_chunk(arrived[place], after), n_fit))

    def integrals(place, before, after):
        here = slice(place, place + 1)
        return exchange_chunks(slots, fit, chunks[here], mine, merged[here], before, after)

    count = len(chunks)
    early = count - MIDDLE_CHUNKS
    for place in range(count + 1):
        if place < count:
            c = chunks[place]
            after = [mine[0]] if place < 2 else [merged[place - 2][0]]
            source = far_blocks if place == 0 else blocks
            picked = pick_blocks(asked[1:], source, c.start, c.count, after)
            arrived.append(
                [lax.ppermute(picked[d - 1], "orb", shifted(n, n - d)) for d in range(1, n)]
            )
        if place > 0:
            after = [picked[0]] if place < count else []
            after += [inverse] if place == PREPARE_AT else []
            after += [arrived[1][j] for j in FIRST_WAITS] if place == 1 else []
            after += merged[-1][1:] if place > SWAP_FIRST else []
            done = place - 1 - INTEGRAL_LAG
            if 0 <= done < early:
                ints = integrals(done, ints, [])
                after.append(ints)
            pass_on(place - 1, after)
    for place in range(max(count - INTEGRAL_LAG, 0), early):
        ints = integrals(place, ints, [merged[-1][0]])
    amplitudes, weights, *sums = middle_step(
        slots, fit, chunks[early:], mine, merged[early:], ints, inverse, off
    )

    first = chunks[-1]
    back = [(first, sums)]
    for c in reversed(cut_rows(first.start, BACK_ROWS)):
        parts, sources = [], []
        for place, chunk in enumerate(chunks[:-1]):
            low = max(c.start, chunk.start)
            high = min(c.start + c.count, chunk.start + chunk.count)
            if low < high:
                parts.append((low, low - chunk.start, high - low))
                sources.append(merged[place][0])
        after = back[-1][1][:1] if CHAIN_GRADIENTS else []
        back.append((c, gradient_chunk(slots, weights, mine[0], parts, sources, after)))

    swap = shifted(n_rep, 1)
    waiting = []
    returned = [
        [sums[0]] + [lax.ppermute(sums[d], "orb", shifted(n, d)) for d in range(1, n)]
        for _, sums in back
    ]
    low = 0
    for high in BACK_GROUPS:
        after = [w[1] for w in waiting[-1:]]
        if high == len(back):
            after = [w[2] for w in waiting[SETTLE_FROM:]]
        here = settle_chunks(asked, returned[low:high], local_orbs, after)
        group = [c for c, _ in back[low:high]]
        waiting.append((group, here, lax.ppermute(here, "rep", swap)))
        low = high
    grads = add_chunks(waiting[:-1], fit_rows)
    grads = add_chunks(waiting[-1:], fit_rows, grads)
    return amplitudes, grads


def solution(mesh):
    placed = (
        P(("groups", "orb"), "fit", None),
        P(("groups", "orb")),
        P(("groups", "orb", "rep"), None),
        P(("groups", "orb", "rep")),
        P(("groups", "orb", "rep"), None, None),
    )
    return jax.shard_map(
        per_device,
        mesh=mesh,
        in_specs=placed,
        out_specs=(P(("groups", "orb", "rep"), None, None), P(("groups", "orb"), "fit", None)),
        check_vma=False,
    )
```
